32 devices in a mesh: cuts: 8 (over z, y), slab: 4 (over x, core).
Axes of the slice: x: 2, y: 2, z: 4, core: 2. Of those that a mesh axis runs over, the one named last changes fastest.
Arguments:
- quasi: bfloat16 [2, 48, 4, 9216], P(None, 'cuts', 'slab'), may hold values from -6 to 6
- counts: int32 [8], replicated, may hold values from 1 to 6, 16 in all
- slot_slice: int32 [48], replicated, may hold values from 0 to 15
- occupation: float32 [48], replicated, may hold values from 0.03125 to 0.25
- filter_coef: float32 [16, 9], replicated, may hold values from -2.5 to 2.5
- trap_index: int32 [4, 9216], P('slab'), may hold values from 0 to 31
- trap_table: float32 [32], replicated, may hold values from 0 to 1.5
- mean_field: float32 [4, 9216], P('slab'), may hold values from -1.5 to 0
- pairing: float32 [4, 9216], P('slab'), may hold values from 0.2 to 1
Outputs:
- normal_density: float32 [4, 9216], P('slab', 'cuts')
- anomalous_density: float32 [4, 9216], P('slab', 'cuts')
- new_mean_field: float32 [4, 9216], P('slab', 'cuts')
- new_pairing: float32 [4, 9216], P('slab', 'cuts')
The draws below stay inside these ranges and needn't reach their ends.
Inputs may be any that keep to these rules, and one draw needn't show every extreme that they name: The live vectors of cut c fill the first counts[c] of its 6 slots; the counts sum to 16 and the largest is exactly 6.
All inputs are finite; a program needn't handle non-finite values.
Results may differ from the reference program's by a relative error of at most 0.0003.
Values may be sent and summed in bfloat16 or wider, within the bound.
A program may use at most 64 MiB of HBM per device.

```python
import math
import jax
import jax.numpy as jnp
import numpy as np
from jax import lax

NX = 96
NY = 96
DEGREE = 8
SLICES = 16
LEVELS = 32
CAP = 6
SLOTS = 48
VECS = 16
NZ = 4
N_CUTS = 8


def draw_quasi(key, part):
    jitter_part = jax.random.normal(jax.random.fold_in(key, 11), (2, SLOTS, NZ, NY * NX), jnp.float32)
    values = jitter_part
    return jnp.clip(values, -6.0, 6.0).astype(jnp.bfloat16)


def draw_filter_coef(key, part):
    baseline = 0.35 * jax.random.normal(jax.random.fold_in(key, 21), (SLICES, DEGREE + 1), jnp.float32)
    values = baseline
    return jnp.clip(values, -2.5, 2.5).astype(jnp.float32)


def draw_trap_table(key, part):
    values = jax.random.uniform(jax.random.fold_in(key, 31), (LEVELS,), jnp.float32, 0.0, 1.5)
    return values.astype(jnp.float32)


def draw_mean_field(key, part):
    values = jax.random.uniform(jax.random.fold_in(key, 41), (NZ, NY * NX), jnp.float32, -1.5, 0.0)
    return values.astype(jnp.float32)


def touch_ends(entries, rng, smallest, top_value):
    shape = entries.shape
    spot = [jax.random.randint(jax.random.fold_in(rng, axis), (), 0, shape[axis]) for axis in range(len(shape))]
    entries = entries.at[tuple(spot)].set(smallest)
    longest = shape.index(max(shape))
    spot[longest] = (spot[longest] + 1) % shape[longest]
    return entries.at[tuple(spot)].set(top_value)


def shard_levels(key, shape, pieces, smallest, high):
    loudness, own = 1.0, jax.random.fold_in(key, 6)
    for dim, shards_of in pieces:
        steps = jnp.exp(jax.random.uniform(jax.random.fold_in(own, dim), (shards_of,), jnp.float32, smallest / len(pieces), high / len(pieces)))
        loudness = loudness * jnp.repeat(steps, shape[dim] // shards_of).reshape([-1 if axis == dim else 1 for axis in range(len(shape))])
    return loudness


def split_up(number_of, total, bound, lean):
    loads = [(1 << 20) // math.isqrt(grade ** lean) + 1 for grade in range(2, number_of + 1)]
    rest, holding = total - bound - (number_of - 1), [1] * (number_of - 1)
    while rest > 0:
        free = [i for i in range(number_of - 1) if holding[i] < bound]
        pool, remaining = sum([loads[i] for i in free]), rest
        for i in free:
            extra = min(bound - holding[i], max(1, remaining * loads[i] // pool), rest)
            holding[i] = holding[i] + extra
            rest = rest - extra
    return np.array([bound] + holding)


def uneven(key, count, total, limit, slope):
    if count == 2:
        one = jax.random.randint(key, (), max(1, total - limit), min(limit, total - 1) + 1)
        return jnp.stack([one, total - one])
    tallies = jnp.asarray(split_up(count, total, limit, slope), jnp.int32)
    pairs = (count - 1) // 2
    source_of, taker = tallies[1:1 + 2 * pairs:2], tallies[2:2 + 2 * pairs:2]
    room = jnp.minimum(source_of - 1, limit - taker)
    passed = jax.random.randint(jax.random.fold_in(key, 1), (pairs,), 0, 1 << 20) % (room + 1)
    tallies = tallies.at[1:1 + 2 * pairs:2].set(source_of - passed).at[2:2 + 2 * pairs:2].set(taker + passed)
    return tallies[jax.random.permutation(jax.random.fold_in(key, 2), count)]


def setup_inputs(seed: int = 0) -> dict:
    arg_keys = jax.random.split(jax.random.key(seed), 10)
    quasi = draw_quasi(jax.random.fold_in(arg_keys[9], 71), 0)
    counts = uneven(arg_keys[1], N_CUTS, VECS, CAP, 2).astype(jnp.int32)
    slot_slice = touch_ends(jax.random.randint(arg_keys[2], (SLOTS,), 0, SLICES), jax.random.fold_in(arg_keys[2], 1), 0, SLICES - 1).astype(jnp.int32)
    occupation = jnp.clip(jnp.exp(jax.random.uniform(arg_keys[3], (SLOTS,), jnp.float32, math.log(0.03125), math.log(0.25))), 0.03125, 0.25)
    filter_coef = draw_filter_coef(jax.random.fold_in(arg_keys[9], 71), 0)
    trap_index = touch_ends(jax.random.randint(arg_keys[5], (NZ, NY * NX), 0, LEVELS), jax.random.fold_in(arg_keys[5], 1), 0, LEVELS - 1).astype(jnp.int32)
    trap_table = draw_trap_table(jax.random.fold_in(arg_keys[9], 71), 0)
    mean_field = draw_mean_field(jax.random.fold_in(arg_keys[9], 71), 0)
    pairing = jnp.clip(0.2 + 0.8 * jax.random.uniform(arg_keys[8], (NZ, NY * NX), jnp.float32) ** shard_levels(arg_keys[8], (NZ, NY * NX), ((0, 4),), -0.2, 0.2), 0.2, 1.0)
    return {"quasi": quasi, "counts": counts, "slot_slice": slot_slice, "occupation": occupation, "filter_coef": filter_coef, "trap_index": trap_index, "trap_table": trap_table, "mean_field": mean_field, "pairing": pairing}


spectral_scale = 8.5
beta_coef = 0.6
chem_level = 1.0
coupling = 1.0
density_floor = 0.05


def combine(field, zpadded, ypadded, potential, pairing):
    column = jnp.arange(field.shape[-1]) % NX
    left_ok = (column > 0).astype(jnp.float32)
    right_ok = (column < NX - 1).astype(jnp.float32)
    xpadded = jnp.pad(field, ((0, 0), (0, 0), (0, 0), (1, 1)))
    beside_all = zpadded[:, :, 2:] + zpadded[:, :, :-2]
    beside_all = beside_all + ypadded[..., 2 * NX:] + ypadded[..., :-2 * NX]
    beside_all = beside_all + xpadded[..., 2:] * right_ok + xpadded[..., :-2] * left_ok
    single = 0.5 * (6.0 * field - beside_all) + potential * field
    upper = single[0] + pairing * field[1]
    lower = pairing * field[0] - single[1]
    return jnp.stack([upper, lower]) / spectral_scale


def apply_block(field, potential, pairing):
    zpadded = jnp.pad(field, ((0, 0), (0, 0), (1, 1), (0, 0)))
    ypadded = jnp.pad(field, ((0, 0), (0, 0), (0, 0), (NX, NX)))
    return combine(field, zpadded, ypadded, potential, pairing)


def chebyshev(vectors, coefs, operator):
    previous = vectors
    current = operator(vectors)
    filtered = coefs[:, 0][None, :, None, None] * previous + coefs[:, 1][None, :, None, None] * current
    for order in range(2, DEGREE + 1):
        following = 2.0 * operator(current) - previous
        filtered = filtered + coefs[:, order][None, :, None, None] * following
        previous, current = current, following
    return filtered


def reference(quasi, counts, slot_slice, occupation, filter_coef, trap_index, trap_table, mean_field, pairing):
    potential = trap_table[trap_index] + mean_field
    slot_ids = jnp.arange(SLOTS).astype(jnp.int32)
    live = ((slot_ids % CAP) < counts[slot_ids // CAP]).astype(jnp.float32)
    weights = occupation * live
    coefs = filter_coef[slot_slice]

    def operator(field):
        return apply_block(field, potential, pairing)

    def step(carry, device):
        start = (device * CAP).astype(jnp.int32)
        block = lax.dynamic_slice_in_dim(quasi, start, CAP, 1).astype(jnp.float32)
        block_coefs = lax.dynamic_slice_in_dim(coefs, start, CAP, 0)
        block_weights = lax.dynamic_slice_in_dim(weights, start, CAP, 0)
        filtered = chebyshev(block, block_coefs, operator)
        normal = jnp.sum(block_weights[:, None, None] * filtered[1] * filtered[1], axis=0)
        anomal = jnp.sum(block_weights[:, None, None] * filtered[0] * filtered[1], axis=0)
        return carry + jnp.stack([normal, anomal]), None

    start_sums = jnp.zeros((2, NZ, NY * NX), jnp.float32)
    sums, unused = lax.scan(step, start_sums, jnp.arange(N_CUTS).astype(jnp.int32))
    normal_density = sums[0]
    anomalous_density = sums[1]
    cube_root = jnp.cbrt(normal_density + density_floor)
    new_mean_field = 0.5 * mean_field + 0.5 * (beta_coef * cube_root * cube_root - chem_level)
    new_pairing = 0.5 * pairing - coupling * anomalous_density
    return normal_density, anomalous_density, new_mean_field, new_pairing
```

```python
import functools

import jax
import jax.numpy as jnp
from jax import lax
from jax.experimental import pallas as pl
from jax.experimental.pallas import tpu as pltpu
from jax.sharding import PartitionSpec as P

NX = 96
DEGREE = 8
LANES = 128
PACK = 4
FLAT = 3
TILE = 16

spectral_scale = 8.5
beta_coef = 0.6
chem_level = 1.0
coupling = 1.0
density_floor = 0.05

MESH = pl.DeviceIdType.MESH


def round_up(value, step):
    return -(-value // step) * step


def plan(n_cuts, n_slab, cap, flat):
    groups = 2 if cap % 2 == 0 and n_slab % 2 == 0 else 1
    pieces = n_slab // groups
    total = flat // (NX * PACK)
    core = total // pieces
    halo = -(-DEGREE // PACK)
    width = min(round_up(core + 2 * halo, TILE), round_up(total, TILE))
    if total >= TILE and core + halo <= TILE:
        width = TILE if pieces <= 2 else width
    starts = [min(max(piece * core - halo, 0), total - width) for piece in range(pieces)]
    return groups, pieces, core, width, starts


def for_planes(count, body):
    chunk = 4 if count % 4 == 0 else 1
    if count == chunk:
        for z in range(chunk):
            body(z)
        return

    def some(i, carry):
        for z in range(chunk):
            body(i * chunk + z)
        return carry

    lax.fori_loop(0, count // chunk, some, 0)


def to_rows(flat_rows, lane):
    p0, p1, p2 = flat_rows
    r0, r1 = pltpu.roll(p0, 32, 1), pltpu.roll(p1, 32, 1)
    s1, s2 = pltpu.roll(p1, 64, 1), pltpu.roll(p2, 64, 1)
    rows = [
        p0,
        jnp.where(lane < 32, r0, r1),
        jnp.where(lane < 64, s1, s2),
        pltpu.roll(p2, 96, 1),
    ]
    return [jnp.where(lane < NX, row, 0.0) for row in rows]


def kernel(
    dims,
    counts,
    slot_slice,
    occupation,
    coef,
    vectors,
    fields,
    out,
    got_q,
    got_f,
    q_rows,
    ab,
    even,
    odd,
    dens,
    parts,
    landed,
    q_send,
    q_recv,
    f_send,
    f_recv,
    p_send,
    p_recv,
):
    n_cuts, nz, groups, pieces, core, width, starts, per_group, share_rows = dims
    cut, slab = lax.axis_index("cuts"), lax.axis_index("slab")
    piece, group = slab // groups, slab % groups
    near = n_cuts // pieces
    home = cut // near
    cap = per_group * groups
    mine = cut * groups + group
    n_sources = n_cuts * groups
    n_targets = near * nz
    keeps_own = (home == piece).astype(jnp.int32)

    barrier = pltpu.get_barrier_semaphore()
    for o in range(1, nz):
        pl.semaphore_signal(
            barrier, inc=1, device_id=(cut, (slab + o) % nz), device_id_type=MESH
        )

    def greet(i, carry):
        source = (mine + i) % n_sources
        c, s = source // groups, home * groups + source % groups

        @pl.when(jnp.logical_or(c != cut, s != slab))
        def _():
            pl.semaphore_signal(barrier, inc=1, device_id=(c, s), device_id_type=MESH)

        return carry

    lax.fori_loop(0, n_sources, greet, 0)
    pl.semaphore_wait(barrier, nz - 1 + n_targets - keeps_own)

    def field_copy(to):
        return pltpu.make_async_remote_copy(
            src_ref=fields.at[to // groups],
            dst_ref=got_f.at[slab],
            send_sem=f_send.at[to],
            recv_sem=f_recv.at[slab],
            device_id=(cut, to),
            device_id_type=MESH,
        )

    def vector_copy(to, slot):
        return pltpu.make_async_remote_copy(
            src_ref=vectors.at[to // groups, to % groups, slot],
            dst_ref=got_q.at[slot, slab],
            send_sem=q_send.at[slot, to],
            recv_sem=q_recv.at[slot, slab],
            device_id=(cut, to),
            device_id_type=MESH,
        )

    others = [(slab + o) % nz for o in range(1, nz)]
    for to in others:
        field_copy(to).start()
        vector_copy(to, 0).start()
    own_f = pltpu.make_async_copy(fields.at[piece], got_f.at[slab], f_recv.at[slab])
    own_f.start()

    def own_q(slot):
        return pltpu.make_async_copy(
            vectors.at[piece, group, slot], got_q.at[slot, slab], q_recv.at[slot, slab]
        )

    own_q(0).start()
    for slot in range(1, per_group):
        for to in others:
            vector_copy(to, slot).start()
        own_q(slot).start()

    lane = lax.broadcasted_iota(jnp.int32, (width, LANES), 1)
    line = lax.broadcasted_iota(jnp.int32, (width, LANES), 0)
    not_first, not_last = line > 0, line < width - 1
    hop = jnp.where(lane < NX, -1.0 / spectral_scale, 0.0).astype(jnp.float32)

    blank = jnp.zeros((2, PACK, width, LANES), jnp.float32)
    for buffer in (even, odd):
        buffer[:, 0] = blank
        buffer[:, nz + 1] = blank
    dens[...] = jnp.zeros(dens.shape, jnp.float32)

    def wait_fields(src):
        pltpu.make_async_remote_copy(
            src_ref=fields.at[piece],
            dst_ref=got_f.at[src],
            send_sem=f_send.at[src],
            recv_sem=f_recv.at[src],
            device_id=(cut, src),
            device_id_type=MESH,
        ).wait_recv()

    own_f.wait()
    for src in others:
        wait_fields(src)

    def unpack_fields(z):
        for which in range(2):
            rows = to_rows([got_f[z, which, j] for j in range(FLAT)], lane)
            for i in range(PACK):
                ab[which, z, i] = rows[i]

    for_planes(nz, unpack_fields)

    def beside(ref, part, z):
        rows = [ref[part, z + 1, i] for i in range(PACK)]
        above = jnp.where(not_first, pltpu.roll(rows[-1], 1, 0), 0.0)
        below = jnp.where(not_last, pltpu.roll(rows[0], width - 1, 0), 0.0)
        padded = [above] + rows + [below]
        sums = []
        for i in range(PACK):
            around = pltpu.roll(rows[i], 1, 1) + pltpu.roll(rows[i], LANES - 1, 1)
            around = around + (padded[i] + padded[i + 2])
            around = around + (ref[part, z, i] + ref[part, z + 2, i])
            sums.append(hop * around)
        return rows, sums

    def twice_operator(ref, z):
        u, near_u = beside(ref, 0, z)
        v, near_v = beside(ref, 1, z)
        results = []
        for i in range(PACK):
            a, b = ab[0, z, i], ab[1, z, i]
            results.append((a * u[i] + b * v[i] + near_u[i], b * u[i] - a * v[i] - near_v[i]))
        return results

    def clenshaw(now, then, scale, first=False):
        def plane(z):
            for i, pair in enumerate(twice_operator(now, z)):
                for part in range(2):
                    value = scale * q_rows[part, z, i] + pair[part]
                    if not first:
                        value = value - then[part, z + 1, i]
                    then[part, z + 1, i] = value

        for_planes(nz, plane)

    def one_slot(slot, carry):
        own_q(slot).wait()
        for src in others:
            pltpu.make_async_remote_copy(
                src_ref=vectors.at[piece, group, slot],
                dst_ref=got_q.at[slot, src],
                send_sem=q_send.at[slot, src],
                recv_sem=q_recv.at[slot, src],
                device_id=(cut, src),
                device_id_type=MESH,
            ).wait_recv()
        index = group * per_group + slot
        number = cut * cap + index
        level = slot_slice[number]
        weight = jnp.where(index < counts[cut], occupation[number], 0.0)
        last = coef[level, DEGREE]

        def unpack(z):
            for part in range(2):
                flat = [got_q[slot, z, j, part].astype(jnp.float32) for j in range(FLAT)]
                rows = to_rows(flat, lane)
                for i in range(PACK):
                    q_rows[part, z, i] = rows[i]
                    even[part, z + 1, i] = last * rows[i]

        for_planes(nz, unpack)
        clenshaw(even, odd, coef[level, DEGREE - 1], first=True)

        def two_steps(k, inner):
            order = DEGREE - 2 - 2 * k
            clenshaw(odd, even, coef[level, order])
            clenshaw(even, odd, coef[level, order - 1])
            return inner

        lax.fori_loop(0, (DEGREE - 2) // 2, two_steps, 0)
        base = coef[level, 0]

        def finish(z):
            for i, pair in enumerate(twice_operator(odd, z)):
                f = [
                    base * q_rows[part, z, i] + 0.5 * pair[part] - even[part, z + 1, i]
                    for part in range(2)
                ]
                heavy = weight * f[1]
                dens[0, z, i] += heavy * f[1]
                dens[1, z, i] += heavy * f[0]

        for_planes(nz, finish)
        return carry

    lax.fori_loop(0, per_group, one_slot, 0)

    start = jnp.int32(starts[0])
    for p in range(1, pieces):
        start = jnp.where(piece == p, starts[p], start)
    inside = piece * core - start

    def pack(z):
        for c in range(near):
            for r in range(share_rows):
                y = c * share_rows + r
                for which in range(2):
                    parts[c, z, pl.ds(which * share_rows + r, 1)] = dens[
                        which, z, y % PACK, pl.ds(inside + y // PACK, 1)
                    ]

    for_planes(nz, pack)

    def part_copy(c, z):
        return pltpu.make_async_remote_copy(
            src_ref=parts.at[c, z],
            dst_ref=landed.at[mine],
            send_sem=p_send.at[c, z],
            recv_sem=p_recv.at[mine],
            device_id=(piece * near + c, z),
            device_id_type=MESH,
        )

    def each_target(act):
        def body(t, carry):
            c, z = (t + cut) % near, (t // near + slab) % nz
            elsewhere = jnp.logical_or(piece * near + c != cut, z != slab)

            @pl.when(elsewhere)
            def _():
                act(part_copy(c, z))

            return carry

        lax.fori_loop(0, n_targets, body, 0)

    each_target(lambda copy: copy.start())

    @pl.when(home == piece)
    def _():
        landed[mine] = parts[cut % near, slab]

    def arrivals(i, carry):
        source = (mine + i) % n_sources
        c, s = source // groups, home * groups + source % groups

        @pl.when(jnp.logical_or(c != cut, s != slab))
        def _():
            pltpu.make_async_remote_copy(
                src_ref=parts.at[0, 0],
                dst_ref=landed.at[source],
                send_sem=p_send.at[0, 0],
                recv_sem=p_recv.at[source],
                device_id=(c, s),
                device_id_type=MESH,
            ).wait_recv()

        return carry

    lax.fori_loop(0, n_sources, arrivals, 0)
    total = landed[0]
    for source in range(1, n_sources):
        total = total + landed[source]
    out[...] = total

    for to in others:
        field_copy(to).wait_send()
        for slot in range(per_group):
            vector_copy(to, slot).wait_send()
    each_target(lambda copy: copy.wait_send())


def body(
    quasi, counts, slot_slice, occupation, filter_coef, trap_index, trap_table, mean_field, pairing
):
    n_cuts, nz = lax.axis_size("cuts"), lax.axis_size("slab")
    cut = lax.axis_index("cuts")
    cap, flat = quasi.shape[1], quasi.shape[3]
    share = flat // n_cuts
    share_rows = share // NX
    groups, pieces, core, width, starts = plan(n_cuts, nz, cap, flat)
    per_group = cap // groups
    n_groups = flat // (NX * PACK)

    levels = jnp.arange(trap_table.shape[0])
    hit = trap_index[None] == levels[:, None, None]
    trap = jnp.sum(jnp.where(hit, trap_table[:, None, None], 0.0), axis=0)
    diagonal = (2.0 / spectral_scale) * (3.0 + trap + mean_field)
    both = jnp.concatenate([diagonal, (2.0 / spectral_scale) * pairing], axis=0)
    both = both.reshape(2, n_groups, FLAT, LANES).transpose(0, 2, 1, 3)
    fields = jnp.stack([both[:, :, s : s + width] for s in starts])

    q = quasi.reshape(2, groups, per_group, n_groups, FLAT, LANES)
    q = q.transpose(1, 2, 4, 0, 3, 5)
    vectors = jnp.stack([q[:, :, :, :, s : s + width] for s in starts])

    rows = round_up(2 * share_rows, 8)
    near = n_cuts // pieces
    dims = (n_cuts, nz, groups, pieces, core, width, starts, per_group, share_rows)
    f32 = jnp.float32
    sums = pl.pallas_call(
        functools.partial(kernel, dims),
        out_shape=jax.ShapeDtypeStruct((rows, LANES), f32),
        in_specs=[pl.BlockSpec(memory_space=pltpu.SMEM)] * 4
        + [pl.BlockSpec(memory_space=pl.ANY)] * 2,
        out_specs=pl.BlockSpec(memory_space=pltpu.VMEM),
        scratch_shapes=[
            pltpu.VMEM((per_group, nz, FLAT, 2, width, LANES), jnp.bfloat16),
            pltpu.VMEM((nz, 2, FLAT, width, LANES), f32),
            pltpu.VMEM((2, nz, PACK, width, LANES), f32),
            pltpu.VMEM((2, nz, PACK, width, LANES), f32),
            pltpu.VMEM((2, nz + 2, PACK, width, LANES), f32),
            pltpu.VMEM((2, nz + 2, PACK, width, LANES), f32),
            pltpu.VMEM((2, nz, PACK, width, LANES), f32),
            pltpu.VMEM((near, nz, rows, LANES), f32),
            pltpu.VMEM((n_cuts * groups, rows, LANES), f32),
            pltpu.SemaphoreType.DMA((per_group, nz)),
            pltpu.SemaphoreType.DMA((per_group, nz)),
            pltpu.SemaphoreType.DMA((nz,)),
            pltpu.SemaphoreType.DMA((nz,)),
            pltpu.SemaphoreType.DMA((near, nz)),
            pltpu.SemaphoreType.DMA((n_cuts * groups,)),
        ],
        compiler_params=pltpu.CompilerParams(
            collective_id=0, has_side_effects=True, vmem_limit_bytes=48 * 1024 * 1024
        ),
    )(counts, slot_slice, occupation, filter_coef, vectors, fields)

    normal_density = sums[:share_rows, :NX].reshape(1, share)
    anomalous_density = sums[share_rows : 2 * share_rows, :NX].reshape(1, share)
    mean_local = lax.dynamic_slice_in_dim(mean_field, cut * share, share, 1)
    pairing_local = lax.dynamic_slice_in_dim(pairing, cut * share, share, 1)
    cube_root = jnp.cbrt(normal_density + density_floor)
    new_mean_field = 0.5 * mean_local + 0.5 * (beta_coef * cube_root * cube_root - chem_level)
    new_pairing = 0.5 * pairing_local - coupling * anomalous_density
    return (normal_density, anomalous_density, new_mean_field, new_pairing)


def solution(mesh):
    return jax.shard_map(
        body,
        mesh=mesh,
        in_specs=(
            P(None, "cuts", "slab", None),
            P(),
            P(),
            P(),
            P(),
            P("slab", None),
            P(),
            P("slab", None),
            P("slab", None),
        ),
        out_specs=(P("slab", "cuts"), P("slab", "cuts"), P("slab", "cuts"), P("slab", "cuts")),
        check_vma=False,
    )
```

```python
import functools

import jax
import jax.numpy as jnp
from jax import lax
from jax.experimental import pallas as pl
from jax.experimental.pallas import tpu as pltpu
from jax.sharding import PartitionSpec as P

NX = 96
DEGREE = 8
LANES = 128
PACK = 4
FLAT = 3
TILE = 16
SUBLANES = 8

spectral_scale = 8.5
beta_coef = 0.6
chem_level = 1.0
coupling = 1.0
density_floor = 0.05

MESH = pl.DeviceIdType.MESH


def round_up(value, step):
    return -(-value // step) * step


def plan(n_cuts, n_slab, cap, flat):
    groups = 2 if cap % 2 == 0 and n_slab % 2 == 0 else 1
    pieces = n_slab // groups
    total = flat // (NX * PACK)
    core = total // pieces
    halo = -(-DEGREE // PACK)
    width = min(round_up(core + halo, TILE), total)
    windows = (total - width) // SUBLANES + 1
    for piece in range(pieces):
        low, high = max(piece * core - halo, 0), min((piece + 1) * core + halo, total)
        start = SUBLANES * min(low // SUBLANES, windows - 1)
        assert start <= low and high <= start + width
    return groups, pieces, core, width, windows


def for_planes(count, body):
    chunk = 4 if count % 4 == 0 else 1
    if count == chunk:
        for z in range(chunk):
            body(z)
        return

    def some(i, carry):
        for z in range(chunk):
            body(i * chunk + z)
        return carry

    lax.fori_loop(0, count // chunk, some, 0)


def to_rows(flat_rows, lane):
    p0, p1, p2 = flat_rows
    r0, r1 = pltpu.roll(p0, 32, 1), pltpu.roll(p1, 32, 1)
    s1, s2 = pltpu.roll(p1, 64, 1), pltpu.roll(p2, 64, 1)
    rows = [
        p0,
        jnp.where(lane < 32, r0, r1),
        jnp.where(lane < 64, s1, s2),
        pltpu.roll(p2, 96, 1),
    ]
    return [jnp.where(lane < NX, row, 0.0) for row in rows]


def kernel(
    dims,
    counts_in,
    slot_slice_in,
    occupation_in,
    coef_in,
    table_in,
    index_in,
    mean_in,
    pairing_in,
    vectors,
    out,
    counts,
    slot_slice,
    occupation,
    coef,
    table,
    index_here,
    mean_here,
    fields,
    got_q,
    got_f,
    q_rows,
    ab,
    even,
    odd,
    dens,
    sibling,
    parts,
    landed,
    load_sem,
    q_send,
    q_recv,
    f_send,
    f_recv,
    s_send,
    s_recv,
    p_send,
    p_recv,
):
    n_cuts, nz, groups, pieces, core, width, windows, per_group, share_rows = dims
    cut, slab = lax.axis_index("cuts"), lax.axis_index("slab")
    near = n_cuts // pieces
    turn = max(near // 2, 1)
    home = cut // near
    cap = per_group * groups
    kept = nz // groups
    halo = -(-DEGREE // PACK)

    def piece_of(s):
        return (s // groups + cut // turn) % pieces

    def window_of(p):
        low = jnp.maximum(p * core - halo, 0)
        return jnp.minimum(low // SUBLANES, windows - 1)

    piece, group = piece_of(slab), slab % groups
    keeps_own = (home == piece).astype(jnp.int32)

    loads = [
        pltpu.make_async_copy(src, dst, load_sem.at[i])
        for i, (src, dst) in enumerate(
            [
                (index_in, index_here),
                (table_in, table),
                (mean_in, mean_here),
                (pairing_in, fields.at[1]),
                (counts_in, counts),
                (slot_slice_in, slot_slice),
                (occupation_in, occupation),
                (coef_in, coef),
            ]
        )
    ]
    for load in loads:
        load.start()

    others = [(slab + o) % nz for o in range(1, nz)]
    barrier = pltpu.get_barrier_semaphore()
    for to in others:
        pl.semaphore_signal(barrier, inc=1, device_id=(cut, to), device_id_type=MESH)

    def source_slab(c):
        return (home + pieces * n_cuts - c // turn) % pieces * groups + group

    for o in range(n_cuts):
        c = (cut + o) % n_cuts
        s = source_slab(c)

        def greet(c=c, s=s):
            pl.semaphore_signal(barrier, inc=1, device_id=(c, s), device_id_type=MESH)

        if o:
            greet()
        else:
            pl.when(s != slab)(greet)

    for load in loads[:4]:
        load.wait()
    hits = index_here[...]
    trap = jnp.zeros(hits.shape, jnp.float32)
    for level in range(table.shape[0]):
        trap = jnp.where(hits == level, table[level], trap)
    fields[0] = (2.0 / spectral_scale) * (3.0 + (trap + mean_here[...]))
    fields[1] = (2.0 / spectral_scale) * fields[1]

    pl.semaphore_wait(barrier, nz - 1 + near * kept - keeps_own)

    def field_copy(to):
        start = pl.multiple_of(window_of(piece_of(to)) * (SUBLANES * FLAT), SUBLANES)
        return pltpu.make_async_remote_copy(
            src_ref=fields.at[:, pl.ds(start, width * FLAT)],
            dst_ref=got_f.at[slab],
            send_sem=f_send.at[to],
            recv_sem=f_recv.at[slab],
            device_id=(cut, to),
            device_id_type=MESH,
        )

    def vector_copy(to, slot):
        return pltpu.make_async_remote_copy(
            src_ref=vectors.at[window_of(piece_of(to)), to % groups, slot],
            dst_ref=got_q.at[slot, slab],
            send_sem=q_send.at[slot, to],
            recv_sem=q_recv.at[slot, slab],
            device_id=(cut, to),
            device_id_type=MESH,
        )

    window = window_of(piece)
    for to in others:
        field_copy(to).start()
    for to in others:
        vector_copy(to, 0).start()
    own_start = pl.multiple_of(window * (SUBLANES * FLAT), SUBLANES)
    own_f = pltpu.make_async_copy(
        fields.at[:, pl.ds(own_start, width * FLAT)], got_f.at[slab], f_recv.at[slab]
    )
    own_f.start()

    def own_q(slot):
        return pltpu.make_async_copy(
            vectors.at[window, group, slot], got_q.at[slot, slab], q_recv.at[slot, slab]
        )

    own_q(0).start()
    for slot in range(1, per_group):
        for to in others:
            vector_copy(to, slot).start()
        own_q(slot).start()
    for load in loads[4:]:
        load.wait()

    lane = lax.broadcasted_iota(jnp.int32, (width, LANES), 1)
    line = lax.broadcasted_iota(jnp.int32, (width, LANES), 0)
    not_first, not_last = line > 0, line < width - 1
    hop = jnp.where(lane < NX, -1.0 / spectral_scale, 0.0).astype(jnp.float32)

    blank = jnp.zeros((2, PACK, width, LANES), jnp.float32)
    for buffer in (even, odd):
        buffer[:, 0] = blank
        buffer[:, nz + 1] = blank
    dens[...] = jnp.zeros(dens.shape, jnp.float32)

    def wait_fields(src):
        pltpu.make_async_remote_copy(
            src_ref=fields.at[:, pl.ds(own_start, width * FLAT)],
            dst_ref=got_f.at[src],
            send_sem=f_send.at[src],
            recv_sem=f_recv.at[src],
            device_id=(cut, src),
            device_id_type=MESH,
        ).wait_recv()

    own_f.wait()
    for src in others:
        wait_fields(src)

    def unpack_fields(z):
        for which in range(2):
            rows = to_rows(
                [got_f[z, which, pl.ds(j, width, stride=FLAT)] for j in range(FLAT)], lane
            )
            for i in range(PACK):
                ab[which, z, i] = rows[i]

    for_planes(nz, unpack_fields)

    def beside(ref, part, z):
        rows = [ref[part, z + 1, i] for i in range(PACK)]
        above = jnp.where(not_first, pltpu.roll(rows[-1], 1, 0), 0.0)
        below = jnp.where(not_last, pltpu.roll(rows[0], width - 1, 0), 0.0)
        padded = [above] + rows + [below]
        sums = []
        for i in range(PACK):
            around = pltpu.roll(rows[i], 1, 1) + pltpu.roll(rows[i], LANES - 1, 1)
            around = around + (padded[i] + padded[i + 2])
            around = around + (ref[part, z, i] + ref[part, z + 2, i])
            sums.append(hop * around)
        return rows, sums

    def twice_operator(ref, z):
        u, near_u = beside(ref, 0, z)
        v, near_v = beside(ref, 1, z)
        results = []
        for i in range(PACK):
            a, b = ab[0, z, i], ab[1, z, i]
            results.append((a * u[i] + b * v[i] + near_u[i], b * u[i] - a * v[i] - near_v[i]))
        return results

    def clenshaw(now, then, scale, first=False):
        def plane(z):
            for i, pair in enumerate(twice_operator(now, z)):
                for part in range(2):
                    value = scale * q_rows[part, z, i] + pair[part]
                    if not first:
                        value = value - then[part, z + 1, i]
                    then[part, z + 1, i] = value

        for_planes(nz, plane)

    def one_slot(slot, carry):
        own_q(slot).wait()
        for src in others:
            pltpu.make_async_remote_copy(
                src_ref=vectors.at[window, group, slot],
                dst_ref=got_q.at[slot, src],
                send_sem=q_send.at[slot, src],
                recv_sem=q_recv.at[slot, src],
                device_id=(cut, src),
                device_id_type=MESH,
            ).wait_recv()
        index = group * per_group + slot
        number = cut * cap + index
        level = slot_slice[number]
        weight = jnp.where(index < counts[cut], occupation[number], 0.0)
        last = coef[level, DEGREE]

        def unpack(z):
            for part in range(2):
                flat = [got_q[slot, z, j, part].astype(jnp.float32) for j in range(FLAT)]
                rows = to_rows(flat, lane)
                for i in range(PACK):
                    q_rows[part, z, i] = rows[i]
                    even[part, z + 1, i] = last * rows[i]

        for_planes(nz, unpack)
        clenshaw(even, odd, coef[level, DEGREE - 1], first=True)

        def two_steps(k, inner):
            order = DEGREE - 2 - 2 * k
            clenshaw(odd, even, coef[level, order])
            clenshaw(even, odd, coef[level, order - 1])
            return inner

        lax.fori_loop(0, (DEGREE - 2) // 2, two_steps, 0)
        base = coef[level, 0]

        def finish(z):
            for i, pair in enumerate(twice_operator(odd, z)):
                f = [
                    base * q_rows[part, z, i] + 0.5 * pair[part] - even[part, z + 1, i]
                    for part in range(2)
                ]
                heavy = weight * f[1]
                dens[z, 0, i] += heavy * f[1]
                dens[z, 1, i] += heavy * f[0]

        for_planes(nz, finish)
        return carry

    lax.fori_loop(0, per_group, one_slot, 0)

    inside = piece * core - window * SUBLANES
    mate = slab + 1 - 2 * group

    def sibling_copy(k):
        return pltpu.make_async_remote_copy(
            src_ref=dens.at[groups * k + 1 - group],
            dst_ref=sibling.at[k],
            send_sem=s_send.at[k],
            recv_sem=s_recv.at[k],
            device_id=(cut, mate),
            device_id_type=MESH,
        )

    def part_copy(c, k):
        return pltpu.make_async_remote_copy(
            src_ref=parts.at[c, k],
            dst_ref=landed.at[cut],
            send_sem=p_send.at[c, k],
            recv_sem=p_recv.at[cut],
            device_id=(piece * near + c, groups * k + group),
            device_id_type=MESH,
        )

    def elsewhere(c, k):
        return jnp.logical_or(piece * near + c != cut, groups * k + group != slab)

    def pack(c, k):
        z = groups * k + group
        if share_rows % PACK == 0:
            step = share_rows // PACK
            spans = [(i, i, c * step, step) for i in range(PACK)]
        else:
            rows = [(r, c * share_rows + r) for r in range(share_rows)]
            spans = [(r, y % PACK, y // PACK, 1) for r, y in rows]
        for which in range(2):
            for r, i, g, n in spans:
                value = dens[z, which, i, pl.ds(inside + g, n)]
                if groups > 1:
                    value = value + sibling[k, which, i, pl.ds(inside + g, n)]
                if n == 1:
                    parts[c, k, pl.ds(which * share_rows + r, 1)] = value
                else:
                    parts[c, k, pl.ds(which * share_rows + r, n, stride=PACK)] = value

    if groups > 1:
        for k in range(kept):
            sibling_copy(k).start()
    for k in range(kept):
        if groups > 1:
            sibling_copy(k).wait_recv()
        for c in range(near):
            pack(c, k)
            pl.when(elsewhere(c, k))(part_copy(c, k).start)

    @pl.when(home == piece)
    def _():
        landed[cut] = parts[cut % near, slab // groups]

    for o in range(n_cuts):
        c = (cut + o) % n_cuts

        def arrive(c=c):
            pltpu.make_async_remote_copy(
                src_ref=parts.at[0, 0],
                dst_ref=landed.at[c],
                send_sem=p_send.at[0, 0],
                recv_sem=p_recv.at[c],
                device_id=(c, source_slab(c)),
                device_id_type=MESH,
            ).wait_recv()

        if o:
            arrive()
        else:
            pl.when(source_slab(c) != slab)(arrive)
    total = landed[0]
    for source in range(1, n_cuts):
        total = total + landed[source]
    out[...] = total

    for to in others:
        field_copy(to).wait_send()
        for slot in range(per_group):
            vector_copy(to, slot).wait_send()
    for k in range(kept):
        if groups > 1:
            sibling_copy(k).wait_send()
        for c in range(near):
            pl.when(elsewhere(c, k))(part_copy(c, k).wait_send)


def body(
    quasi, counts, slot_slice, occupation, filter_coef, trap_index, trap_table, mean_field, pairing
):
    n_cuts, nz = lax.axis_size("cuts"), lax.axis_size("slab")
    cut = lax.axis_index("cuts")
    cap, flat = quasi.shape[1], quasi.shape[3]
    share = flat // n_cuts
    share_rows = share // NX
    groups, pieces, core, width, windows = plan(n_cuts, nz, cap, flat)
    per_group = cap // groups
    n_groups = flat // (NX * PACK)

    q = quasi.reshape(2, groups, per_group, n_groups, FLAT, LANES)
    q = q.transpose(1, 2, 4, 0, 3, 5)
    starts = [SUBLANES * w for w in range(windows)]
    vectors = jnp.stack([q[:, :, :, :, s : s + width] for s in starts])

    rows = round_up(2 * share_rows, SUBLANES)
    near = n_cuts // pieces
    kept = nz // groups
    dims = (n_cuts, nz, groups, pieces, core, width, windows, per_group, share_rows)
    f32, i32 = jnp.float32, jnp.int32
    tall = (flat // LANES, LANES)
    slots = slot_slice.shape[0]
    sums = pl.pallas_call(
        functools.partial(kernel, dims),
        out_shape=jax.ShapeDtypeStruct((rows, LANES), f32),
        in_specs=[pl.BlockSpec(memory_space=pltpu.HBM)] * 8
        + [pl.BlockSpec(memory_space=pl.ANY)],
        out_specs=pl.BlockSpec(memory_space=pltpu.VMEM),
        scratch_shapes=[
            pltpu.SMEM((n_cuts,), i32),
            pltpu.SMEM((slots,), i32),
            pltpu.SMEM((slots,), f32),
            pltpu.SMEM(filter_coef.shape, f32),
            pltpu.SMEM(trap_table.shape, f32),
            pltpu.VMEM(tall, i32),
            pltpu.VMEM(tall, f32),
            pltpu.VMEM((2, *tall), f32),
            pltpu.VMEM((per_group, nz, FLAT, 2, width, LANES), jnp.bfloat16),
            pltpu.VMEM((nz, 2, FLAT * width, LANES), f32),
            pltpu.VMEM((2, nz, PACK, width, LANES), f32),
            pltpu.VMEM((2, nz, PACK, width, LANES), f32),
            pltpu.VMEM((2, nz + 2, PACK, width, LANES), f32),
            pltpu.VMEM((2, nz + 2, PACK, width, LANES), f32),
            pltpu.VMEM((nz, 2, PACK, width, LANES), f32),
            pltpu.VMEM((kept, 2, PACK, width, LANES), f32),
            pltpu.VMEM((near, kept, rows, LANES), f32),
            pltpu.VMEM((n_cuts, rows, LANES), f32),
            pltpu.SemaphoreType.DMA((8,)),
            pltpu.SemaphoreType.DMA((per_group, nz)),
            pltpu.SemaphoreType.DMA((per_group, nz)),
            pltpu.SemaphoreType.DMA((nz,)),
            pltpu.SemaphoreType.DMA((nz,)),
            pltpu.SemaphoreType.DMA((kept,)),
            pltpu.SemaphoreType.DMA((kept,)),
            pltpu.SemaphoreType.DMA((near, kept)),
            pltpu.SemaphoreType.DMA((n_cuts,)),
        ],
        compiler_params=pltpu.CompilerParams(
            collective_id=0, has_side_effects=True, vmem_limit_bytes=48 * 1024 * 1024
        ),
    )(
        counts,
        slot_slice,
        occupation,
        filter_coef,
        trap_table,
        trap_index.reshape(tall),
        mean_field.reshape(tall),
        pairing.reshape(tall),
        vectors,
    )

    flat_sums = sums[: 2 * share_rows, :NX].reshape(2, share)
    normal_density, anomalous_density = flat_sums[:1], flat_sums[1:]
    mean_local = lax.dynamic_slice_in_dim(mean_field, cut * share, share, 1)
    pairing_local = lax.dynamic_slice_in_dim(pairing, cut * share, share, 1)
    cube_root = jnp.cbrt(normal_density + density_floor)
    new_mean_field = 0.5 * mean_local + 0.5 * (beta_coef * cube_root * cube_root - chem_level)
    new_pairing = 0.5 * pairing_local - coupling * anomalous_density
    return (normal_density, anomalous_density, new_mean_field, new_pairing)


def solution(mesh):
    return jax.shard_map(
        body,
        mesh=mesh,
        in_specs=(
            P(None, "cuts", "slab", None),
            P(),
            P(),
            P(),
            P(),
            P("slab", None),
            P(),
            P("slab", None),
            P("slab", None),
        ),
        out_specs=(P("slab", "cuts"), P("slab", "cuts"), P("slab", "cuts"), P("slab", "cuts")),
        check_vma=False,
    )
```

```python
import functools

import jax
import jax.numpy as jnp
from jax import lax
from jax.experimental import pallas as pl
from jax.experimental.pallas import tpu as pltpu
from jax.sharding import PartitionSpec as P

NX = 96
DEGREE = 8
LANES = 128
PACK = 4
FLAT = 3
TILE = 16
SUBLANES = 8
VMEM_BYTES = 65000 * 1024

spectral_scale = 8.5
beta_coef = 0.6
chem_level = 1.0
coupling = 1.0
density_floor = 0.05

MESH = pl.DeviceIdType.MESH


def round_up(value, step):
    return -(-value // step) * step


def plan(n_cuts, n_slab, cap, flat):
    groups = 2 if cap % 2 == 0 and n_slab % 2 == 0 else 1
    pieces = n_slab // groups
    total = flat // (NX * PACK)
    core = total // pieces
    halo = -(-DEGREE // PACK)
    width = min(round_up(core + halo, TILE), total)
    windows = (total - width) // SUBLANES + 1
    for piece in range(pieces):
        low, high = max(piece * core - halo, 0), min((piece + 1) * core + halo, total)
        start = SUBLANES * min(low // SUBLANES, windows - 1)
        assert start <= low and high <= start + width
    return groups, pieces, core, width, windows


def for_planes(count, body):
    chunk = 4 if count % 4 == 0 else 1
    if count == chunk:
        for z in range(chunk):
            body(z)
        return

    def some(i, carry):
        for z in range(chunk):
            body(i * chunk + z)
        return carry

    lax.fori_loop(0, count // chunk, some, 0)


def to_rows(flat_rows, lane):
    p0, p1, p2 = flat_rows
    r0, r1 = pltpu.roll(p0, 32, 1), pltpu.roll(p1, 32, 1)
    s1, s2 = pltpu.roll(p1, 64, 1), pltpu.roll(p2, 64, 1)
    rows = [
        p0,
        jnp.where(lane < 32, r0, r1),
        jnp.where(lane < 64, s1, s2),
        pltpu.roll(p2, 96, 1),
    ]
    return [jnp.where(lane < NX, row, 0.0) for row in rows]


def kernel(
    dims,
    counts_in,
    slot_slice_in,
    occupation_in,
    coef_in,
    table_in,
    index_in,
    mean_in,
    pairing_in,
    vectors,
    out,
    counts,
    slot_slice,
    occupation,
    coef,
    table,
    index_here,
    mean_here,
    fields,
    got_q,
    got_f,
    wide,
    q_rows,
    ab,
    even,
    odd,
    dens,
    sibling,
    parts,
    landed,
    load_sem,
    q_send,
    q_recv,
    f_send,
    f_recv,
    s_send,
    s_recv,
    p_send,
    p_recv,
):
    n_cuts, nz, groups, pieces, core, width, windows, per_group, share_rows = dims
    cut, slab = lax.axis_index("cuts"), lax.axis_index("slab")
    near = n_cuts // pieces
    turn = max(near // 2, 1)
    home = cut // near
    cap = per_group * groups
    kept = nz // groups
    halo = -(-DEGREE // PACK)

    def piece_of(s):
        return (s // groups + cut // turn) % pieces

    def window_of(p):
        low = jnp.maximum(p * core - halo, 0)
        return jnp.minimum(low // SUBLANES, windows - 1)

    piece, group = piece_of(slab), slab % groups
    keeps_own = (home == piece).astype(jnp.int32)

    others = [(slab + o) % nz for o in range(1, nz)]
    barrier = pltpu.get_barrier_semaphore()
    for to in others:
        pl.semaphore_signal(barrier, inc=1, device_id=(cut, to), device_id_type=MESH)

    def source_slab(c):
        return (home + pieces * n_cuts - c // turn) % pieces * groups + group

    for o in range(n_cuts):
        c = (cut + o) % n_cuts
        s = source_slab(c)

        def greet(c=c, s=s):
            pl.semaphore_signal(barrier, inc=1, device_id=(c, s), device_id_type=MESH)

        if o:
            greet()
        else:
            pl.when(s != slab)(greet)

    loads = [
        pltpu.make_async_copy(src, dst, load_sem.at[i])
        for i, (src, dst) in enumerate(
            [
                (index_in, index_here),
                (table_in, table),
                (mean_in, mean_here),
                (pairing_in, fields.at[1]),
                (counts_in, counts),
                (slot_slice_in, slot_slice),
                (occupation_in, occupation),
                (coef_in, coef),
            ]
        )
    ]
    for load in loads:
        load.start()

    for load in loads[:4]:
        load.wait()
    hits = index_here[...]
    trap = jnp.zeros(hits.shape, jnp.float32)
    for level in range(table.shape[0]):
        trap = jnp.where(hits == level, table[level], trap)
    fields[0] = (2.0 / spectral_scale) * (3.0 + (trap + mean_here[...]))
    fields[1] = (2.0 / spectral_scale) * fields[1]

    pl.semaphore_wait(barrier, nz - 1 + near * kept - keeps_own)

    mate = slab + 1 - 2 * group

    def passed_on(src):
        return pltpu.make_async_remote_copy(
            src_ref=got_f.at[src],
            dst_ref=got_f.at[src],
            send_sem=f_send.at[nz + src],
            recv_sem=f_recv.at[src],
            device_id=(cut, mate),
            device_id_type=MESH,
        )

    def field_copy(to):
        start = pl.multiple_of(window_of(piece_of(to)) * (SUBLANES * FLAT), SUBLANES)
        return pltpu.make_async_remote_copy(
            src_ref=fields.at[:, pl.ds(start, width * FLAT)],
            dst_ref=got_f.at[slab],
            send_sem=f_send.at[to],
            recv_sem=f_recv.at[slab],
            device_id=(cut, to),
            device_id_type=MESH,
        )

    def vector_copy(to, slot):
        return pltpu.make_async_remote_copy(
            src_ref=vectors.at[
                to % groups * per_group + slot, pl.ds(window_of(piece_of(to)) * (SUBLANES * FLAT), width * FLAT)
            ],
            dst_ref=got_q.at[slot, slab],
            send_sem=q_send.at[slot, to],
            recv_sem=q_recv.at[slot, slab],
            device_id=(cut, to),
            device_id_type=MESH,
        )

    window = window_of(piece)
    alike = [(slab + o) % nz for o in range(groups, nz, groups)]
    direct = alike + ([mate] if groups > 1 else [])
    for to in direct:
        field_copy(to).start()
    for to in others:
        vector_copy(to, 0).start()
    own_start = pl.multiple_of(window * (SUBLANES * FLAT), SUBLANES)
    own_f = pltpu.make_async_copy(
        fields.at[:, pl.ds(own_start, width * FLAT)], got_f.at[slab], f_recv.at[slab]
    )
    own_f.start()

    def own_q(slot):
        return pltpu.make_async_copy(
            vectors.at[group * per_group + slot, pl.ds(own_start, width * FLAT)],
            got_q.at[slot, slab],
            q_recv.at[slot, slab],
        )

    own_q(0).start()
    for slot in range(1, per_group):
        for to in others:
            vector_copy(to, slot).start()
        own_q(slot).start()
    for load in loads[4:]:
        load.wait()

    lane = lax.broadcasted_iota(jnp.int32, (width, LANES), 1)
    line = lax.broadcasted_iota(jnp.int32, (width, LANES), 0)
    not_first, not_last = line > 0, line < width - 1
    hop = jnp.where(lane < NX, -1.0 / spectral_scale, 0.0).astype(jnp.float32)

    blank = jnp.zeros((2, PACK, width, LANES), jnp.float32)
    for buffer in (even, odd):
        buffer[:, 0] = blank
        buffer[:, nz + 1] = blank
    dens[...] = jnp.zeros(dens.shape, jnp.float32)

    def wait_fields(src):
        pltpu.make_async_remote_copy(
            src_ref=fields.at[:, pl.ds(own_start, width * FLAT)],
            dst_ref=got_f.at[src],
            send_sem=f_send.at[src],
            recv_sem=f_recv.at[src],
            device_id=(cut, src),
            device_id_type=MESH,
        ).wait_recv()

    for src in alike:
        wait_fields(src)
        if groups > 1:
            passed_on(src).start()
    own_f.wait()
    if groups > 1:
        wait_fields(mate)
        for src in alike:
            wait_fields(src + 1 - 2 * group)

    def unpack_fields(z):
        for which in range(2):
            rows = to_rows(
                [got_f[z, which, pl.ds(j, width, stride=FLAT)] for j in range(FLAT)], lane
            )
            for i in range(PACK):
                ab[which, z, i] = rows[i]

    for_planes(nz, unpack_fields)

    def beside(ref, part, z):
        rows = [ref[part, z + 1, i] for i in range(PACK)]
        above = jnp.where(not_first, pltpu.roll(rows[-1], 1, 0), 0.0)
        below = jnp.where(not_last, pltpu.roll(rows[0], width - 1, 0), 0.0)
        padded = [above] + rows + [below]
        sums = []
        for i in range(PACK):
            around = pltpu.roll(rows[i], 1, 1) + pltpu.roll(rows[i], LANES - 1, 1)
            around = around + (padded[i] + padded[i + 2])
            around = around + (ref[part, z, i] + ref[part, z + 2, i])
            sums.append(hop * around)
        return rows, sums

    def twice_operator(ref, z):
        u, near_u = beside(ref, 0, z)
        v, near_v = beside(ref, 1, z)
        results = []
        for i in range(PACK):
            a, b = ab[0, z, i], ab[1, z, i]
            results.append((a * u[i] + b * v[i] + near_u[i], b * u[i] - a * v[i] - near_v[i]))
        return results

    def clenshaw(now, then, scale, first=False):
        def plane(z):
            for i, pair in enumerate(twice_operator(now, z)):
                for part in range(2):
                    value = scale * q_rows[part, z, i] + pair[part]
                    if not first:
                        value = value - then[part, z + 1, i]
                    then[part, z + 1, i] = value

        for_planes(nz, plane)

    def sibling_copy(k):
        return pltpu.make_async_remote_copy(
            src_ref=dens.at[groups * k + 1 - group],
            dst_ref=sibling.at[k],
            send_sem=s_send.at[k],
            recv_sem=s_recv.at[k],
            device_id=(cut, mate),
            device_id_type=MESH,
        )

    def one_slot(slot, carry):
        own_q(slot).wait()
        for src in others:
            pltpu.make_async_remote_copy(
                src_ref=vectors.at[slot, pl.ds(own_start, width * FLAT)],
                dst_ref=got_q.at[slot, src],
                send_sem=q_send.at[slot, src],
                recv_sem=q_recv.at[slot, src],
                device_id=(cut, src),
                device_id_type=MESH,
            ).wait_recv()
        index = group * per_group + slot
        number = cut * cap + index
        level = slot_slice[number]
        weight = jnp.where(index < counts[cut], occupation[number], 0.0)
        last = coef[level, DEGREE]

        def unpack(z):
            for r in range(width * FLAT):
                wide[z, pl.ds(2 * r, 2)] = got_q[slot, z, r].astype(jnp.float32)
            for part in range(2):
                flat = [
                    wide[z, pl.ds(2 * j + part, width, stride=2 * FLAT)] for j in range(FLAT)
                ]
                rows = to_rows(flat, lane)
                for i in range(PACK):
                    q_rows[part, z, i] = rows[i]
                    even[part, z + 1, i] = last * rows[i]

        for_planes(nz, unpack)
        clenshaw(even, odd, coef[level, DEGREE - 1], first=True)

        def two_steps(k, inner):
            order = DEGREE - 2 - 2 * k
            clenshaw(odd, even, coef[level, order])
            clenshaw(even, odd, coef[level, order - 1])
            return inner

        lax.fori_loop(0, (DEGREE - 2) // 2, two_steps, 0)
        base = coef[level, 0]

        def finish(z):
            for i, pair in enumerate(twice_operator(odd, z)):
                f = [
                    base * q_rows[part, z, i] + 0.5 * pair[part] - even[part, z + 1, i]
                    for part in range(2)
                ]
                heavy = weight * f[1]
                dens[z, 0, i] += heavy * f[1]
                dens[z, 1, i] += heavy * f[0]

        if groups == 1:
            for_planes(nz, finish)
            return carry
        for k in range(kept):
            finish(groups * k + 1 - group)
            pl.when(slot == per_group - 1)(sibling_copy(k).start)
        for k in range(kept):
            finish(groups * k + group)
        return carry

    lax.fori_loop(0, per_group, one_slot, 0)

    inside = piece * core - window * SUBLANES
    def part_copy(c, k):
        return pltpu.make_async_remote_copy(
            src_ref=parts.at[c, k],
            dst_ref=landed.at[cut],
            send_sem=p_send.at[c, k],
            recv_sem=p_recv.at[cut],
            device_id=(piece * near + c, groups * k + group),
            device_id_type=MESH,
        )

    def elsewhere(c, k):
        return jnp.logical_or(piece * near + c != cut, groups * k + group != slab)

    def pack(c, k):
        z = groups * k + group
        if share_rows % PACK == 0:
            step = share_rows // PACK
            spans = [(i, i, c * step, step) for i in range(PACK)]
        else:
            rows = [(r, c * share_rows + r) for r in range(share_rows)]
            spans = [(r, y % PACK, y // PACK, 1) for r, y in rows]
        for which in range(2):
            for r, i, g, n in spans:
                value = dens[z, which, i, pl.ds(inside + g, n)]
                if groups > 1:
                    value = value + sibling[k, which, i, pl.ds(inside + g, n)]
                if n == 1:
                    parts[c, k, pl.ds(which * share_rows + r, 1)] = value
                else:
                    parts[c, k, pl.ds(which * share_rows + r, n, stride=PACK)] = value

    for k in range(kept):
        if groups > 1:
            sibling_copy(k).wait_recv()
        for c in range(near):
            pack(c, k)
            pl.when(elsewhere(c, k))(part_copy(c, k).start)

    @pl.when(home == piece)
    def _():
        landed[cut] = parts[cut % near, slab // groups]

    for o in range(n_cuts):
        c = (cut + o) % n_cuts

        def arrive(c=c):
            pltpu.make_async_remote_copy(
                src_ref=parts.at[0, 0],
                dst_ref=landed.at[c],
                send_sem=p_send.at[0, 0],
                recv_sem=p_recv.at[c],
                device_id=(c, source_slab(c)),
                device_id_type=MESH,
            ).wait_recv()

        if o:
            arrive()
        else:
            pl.when(source_slab(c) != slab)(arrive)
    total = landed[0]
    for source in range(1, n_cuts):
        total = total + landed[source]
    out[...] = total

    for to in direct:
        field_copy(to).wait_send()
    if groups > 1:
        for src in alike:
            passed_on(src).wait_send()
    for to in others:
        for slot in range(per_group):
            vector_copy(to, slot).wait_send()
    for k in range(kept):
        if groups > 1:
            sibling_copy(k).wait_send()
        for c in range(near):
            pl.when(elsewhere(c, k))(part_copy(c, k).wait_send)


def body(
    quasi, counts, slot_slice, occupation, filter_coef, trap_index, trap_table, mean_field, pairing
):
    n_cuts, nz = lax.axis_size("cuts"), lax.axis_size("slab")
    cut = lax.axis_index("cuts")
    cap, flat = quasi.shape[1], quasi.shape[3]
    share = flat // n_cuts
    share_rows = share // NX
    groups, pieces, core, width, windows = plan(n_cuts, nz, cap, flat)
    per_group = cap // groups
    vectors = quasi.reshape(2, cap, flat // LANES, LANES).transpose(1, 2, 0, 3)

    rows = round_up(2 * share_rows, SUBLANES)
    near = n_cuts // pieces
    kept = nz // groups
    dims = (n_cuts, nz, groups, pieces, core, width, windows, per_group, share_rows)
    f32, i32 = jnp.float32, jnp.int32
    tall = (flat // LANES, LANES)
    slots = slot_slice.shape[0]
    sums = pl.pallas_call(
        functools.partial(kernel, dims),
        out_shape=jax.ShapeDtypeStruct((rows, LANES), f32),
        in_specs=[pl.BlockSpec(memory_space=pltpu.HBM)] * 8
        + [pl.BlockSpec(memory_space=pl.ANY)],
        out_specs=pl.BlockSpec(memory_space=pltpu.VMEM),
        scratch_shapes=[
            pltpu.SMEM((n_cuts,), i32),
            pltpu.SMEM((slots,), i32),
            pltpu.SMEM((slots,), f32),
            pltpu.SMEM(filter_coef.shape, f32),
            pltpu.SMEM(trap_table.shape, f32),
            pltpu.VMEM(tall, i32),
            pltpu.VMEM(tall, f32),
            pltpu.VMEM((2, *tall), f32),
            pltpu.VMEM((per_group, nz, FLAT * width, 2, LANES), jnp.bfloat16),
            pltpu.VMEM((nz, 2, FLAT * width, LANES), f32),
            pltpu.VMEM((nz, 2 * FLAT * width, LANES), f32),
            pltpu.VMEM((2, nz, PACK, width, LANES), f32),
            pltpu.VMEM((2, nz, PACK, width, LANES), f32),
            pltpu.VMEM((2, nz + 2, PACK, width, LANES), f32),
            pltpu.VMEM((2, nz + 2, PACK, width, LANES), f32),
            pltpu.VMEM((nz, 2, PACK, width, LANES), f32),
            pltpu.VMEM((kept, 2, PACK, width, LANES), f32),
            pltpu.VMEM((near, kept, rows, LANES), f32),
            pltpu.VMEM((n_cuts, rows, LANES), f32),
            pltpu.SemaphoreType.DMA((8,)),
            pltpu.SemaphoreType.DMA((per_group, nz)),
            pltpu.SemaphoreType.DMA((per_group, nz)),
            pltpu.SemaphoreType.DMA((2 * nz,)),
            pltpu.SemaphoreType.DMA((nz,)),
            pltpu.SemaphoreType.DMA((kept,)),
            pltpu.SemaphoreType.DMA((kept,)),
            pltpu.SemaphoreType.DMA((near, kept)),
            pltpu.SemaphoreType.DMA((n_cuts,)),
        ],
        compiler_params=pltpu.CompilerParams(
            collective_id=0, has_side_effects=True, vmem_limit_bytes=VMEM_BYTES
        ),
    )(
        counts,
        slot_slice,
        occupation,
        filter_coef,
        trap_table,
        trap_index.reshape(tall),
        mean_field.reshape(tall),
        pairing.reshape(tall),
        vectors,
    )

    flat_sums = sums[: 2 * share_rows, :NX].reshape(2, share)
    normal_density, anomalous_density = flat_sums[:1], flat_sums[1:]
    mean_local = lax.dynamic_slice_in_dim(mean_field, cut * share, share, 1)
    pairing_local = lax.dynamic_slice_in_dim(pairing, cut * share, share, 1)
    cube_root = jnp.cbrt(normal_density + density_floor)
    new_mean_field = 0.5 * mean_local + 0.5 * (beta_coef * cube_root * cube_root - chem_level)
    new_pairing = 0.5 * pairing_local - coupling * anomalous_density
    return (normal_density, anomalous_density, new_mean_field, new_pairing)


def solution(mesh):
    return jax.shard_map(
        body,
        mesh=mesh,
        in_specs=(
            P(None, "cuts", "slab", None),
            P(),
            P(),
            P(),
            P(),
            P("slab", None),
            P(),
            P("slab", None),
            P("slab", None),
        ),
        out_specs=(P("slab", "cuts"), P("slab", "cuts"), P("slab", "cuts"), P("slab", "cuts")),
        check_vma=False,
    )
```

```python
import functools

import jax
import jax.numpy as jnp
from jax import lax
from jax.experimental import pallas as pl
from jax.experimental.pallas import tpu as pltpu
from jax.sharding import PartitionSpec as P

NX = 96
DEGREE = 8
LANES = 128
PACK = 4
FLAT = 3
TILE = 16
SUBLANES = 8
VMEM_BYTES = 65000 * 1024

spectral_scale = 8.5
beta_coef = 0.6
chem_level = 1.0
coupling = 1.0
density_floor = 0.05

MESH = pl.DeviceIdType.MESH


def round_up(value, step):
    return -(-value // step) * step


def plan(n_cuts, n_slab, cap, flat):
    groups = 2 if cap % 2 == 0 and n_slab % 2 == 0 else 1
    pieces = n_slab // groups
    total = flat // (NX * PACK)
    core = total // pieces
    halo = -(-DEGREE // PACK)
    width = min(round_up(core + halo, TILE), total)
    windows = (total - width) // SUBLANES + 1
    for piece in range(pieces):
        low, high = max(piece * core - halo, 0), min((piece + 1) * core + halo, total)
        start = SUBLANES * min(low // SUBLANES, windows - 1)
        assert start <= low and high <= start + width
    return groups, pieces, core, width, windows


def for_planes(count, body):
    chunk = 4 if count % 4 == 0 else 1
    if count == chunk:
        for z in range(chunk):
            body(z)
        return

    def some(i, carry):
        for z in range(chunk):
            body(i * chunk + z)
        return carry

    lax.fori_loop(0, count // chunk, some, 0)


def to_rows(flat_rows):
    p0, p1, p2 = flat_rows
    lane = lax.broadcasted_iota(jnp.int32, p0.shape, 1)
    r0, r1 = pltpu.roll(p0, 32, 1), pltpu.roll(p1, 32, 1)
    s1, s2 = pltpu.roll(p1, 64, 1), pltpu.roll(p2, 64, 1)
    rows = [
        p0,
        jnp.where(lane < 32, r0, r1),
        jnp.where(lane < 64, s1, s2),
        pltpu.roll(p2, 96, 1),
    ]
    return [jnp.where(lane < NX, row, 0.0) for row in rows]


def kernel(
    dims,
    counts_in,
    slot_slice_in,
    occupation_in,
    coef_in,
    table_in,
    index_in,
    mean_in,
    pairing_in,
    vectors,
    out,
    counts,
    slot_slice,
    occupation,
    coef,
    table,
    index_here,
    mean_here,
    pairing_here,
    local_rows,
    fields,
    got_q,
    got_f,
    wide,
    q_rows,
    ab,
    even,
    odd,
    dens,
    sibling,
    parts,
    landed,
    load_sem,
    q_send,
    q_recv,
    f_send,
    f_recv,
    s_send,
    s_recv,
    p_send,
    p_recv,
):
    n_cuts, nz, groups, pieces, core, width, windows, per_group, share_rows = dims
    cut, slab = lax.axis_index("cuts"), lax.axis_index("slab")
    near = n_cuts // pieces
    turn = max(near // 2, 1)
    home = cut // near
    cap = per_group * groups
    kept = nz // groups
    halo = -(-DEGREE // PACK)

    def piece_of(s):
        return (s // groups + cut // turn) % pieces

    def window_of(p):
        low = jnp.maximum(p * core - halo, 0)
        return jnp.minimum(low // SUBLANES, windows - 1)

    piece, group = piece_of(slab), slab % groups
    keeps_own = (home == piece).astype(jnp.int32)

    others = [(slab + o) % nz for o in range(1, nz)]
    barrier = pltpu.get_barrier_semaphore()
    for to in others:
        pl.semaphore_signal(barrier, inc=1, device_id=(cut, to), device_id_type=MESH)

    loads = [
        pltpu.make_async_copy(src, dst, load_sem.at[i])
        for i, (src, dst) in enumerate(
            [
                (index_in, index_here),
                (table_in, table),
                (mean_in, mean_here),
                (pairing_in, pairing_here),
                (counts_in, counts),
                (slot_slice_in, slot_slice),
                (occupation_in, occupation),
                (coef_in, coef),
            ]
        )
    ]
    for load in loads:
        load.start()

    def source_slab(c):
        return (home + pieces * n_cuts - c // turn) % pieces * groups + group

    for o in range(n_cuts):
        c = (cut + o) % n_cuts
        s = source_slab(c)

        def greet(c=c, s=s):
            pl.semaphore_signal(barrier, inc=1, device_id=(c, s), device_id_type=MESH)

        if o:
            greet()
        else:
            pl.when(s != slab)(greet)

    for load in loads[:4]:
        load.wait()
    hits = index_here[...]
    trap = jnp.zeros(hits.shape, jnp.float32)
    for level in range(table.shape[0]):
        trap = jnp.where(hits == level, table[level], trap)
    fields[0] = (2.0 / spectral_scale) * (3.0 + (trap + mean_here[...]))
    fields[1] = (2.0 / spectral_scale) * pairing_here[...]

    pl.semaphore_wait(barrier, nz - 1 + near * kept - keeps_own)

    mate = slab + 1 - 2 * group

    def passed_on(src):
        return pltpu.make_async_remote_copy(
            src_ref=got_f.at[src],
            dst_ref=got_f.at[src],
            send_sem=f_send.at[nz + src],
            recv_sem=f_recv.at[src],
            device_id=(cut, mate),
            device_id_type=MESH,
        )

    def field_copy(to):
        start = pl.multiple_of(window_of(piece_of(to)) * (SUBLANES * FLAT), SUBLANES)
        return pltpu.make_async_remote_copy(
            src_ref=fields.at[:, pl.ds(start, width * FLAT)],
            dst_ref=got_f.at[slab],
            send_sem=f_send.at[to],
            recv_sem=f_recv.at[slab],
            device_id=(cut, to),
            device_id_type=MESH,
        )

    def vector_copy(to, slot):
        start = window_of(piece_of(to)) * (SUBLANES * FLAT)
        return pltpu.make_async_remote_copy(
            src_ref=vectors.at[to % groups * per_group + slot, pl.ds(start, width * FLAT)],
            dst_ref=got_q.at[slot, slab],
            send_sem=q_send.at[slot, to],
            recv_sem=q_recv.at[slot, slab],
            device_id=(cut, to),
            device_id_type=MESH,
        )

    window = window_of(piece)
    alike = [(slab + o) % nz for o in range(groups, nz, groups)]
    direct = alike + ([mate] if groups > 1 else [])
    for to in direct:
        field_copy(to).start()
    for to in others:
        vector_copy(to, 0).start()
    own_start = pl.multiple_of(window * (SUBLANES * FLAT), SUBLANES)
    own_f = pltpu.make_async_copy(
        fields.at[:, pl.ds(own_start, width * FLAT)], got_f.at[slab], f_recv.at[slab]
    )
    own_f.start()

    def own_q(slot):
        return pltpu.make_async_copy(
            vectors.at[group * per_group + slot, pl.ds(own_start, width * FLAT)],
            got_q.at[slot, slab],
            q_recv.at[slot, slab],
        )

    own_q(0).start()
    for load in loads[4:]:
        load.wait()

    lane = lax.broadcasted_iota(jnp.int32, (width, LANES), 1)
    line = lax.broadcasted_iota(jnp.int32, (width, LANES), 0)
    not_first, not_last = line > 0, line < width - 1
    hop = jnp.where(lane < NX, -1.0 / spectral_scale, 0.0).astype(jnp.float32)

    blank = jnp.zeros((2, PACK, width, LANES), jnp.float32)
    for buffer in (even, odd):
        buffer[:, 0] = blank
        buffer[:, nz + 1] = blank
    dens[...] = jnp.zeros(dens.shape, jnp.float32)

    for part, here in enumerate((mean_here, pairing_here)):
        count = here.shape[0] // FLAT
        rows = to_rows([here[pl.ds(j, count, stride=FLAT)] for j in range(FLAT)])
        for i in range(PACK):
            local_rows[part, i] = rows[i]
        for r in range(share_rows):
            y = cut * share_rows + r
            out[part, pl.ds(2 * share_rows + r, 1)] = local_rows[part, y % PACK, pl.ds(y // PACK, 1)]

    def wait_fields(src):
        pltpu.make_async_remote_copy(
            src_ref=fields.at[:, pl.ds(own_start, width * FLAT)],
            dst_ref=got_f.at[src],
            send_sem=f_send.at[src],
            recv_sem=f_recv.at[src],
            device_id=(cut, src),
            device_id_type=MESH,
        ).wait_recv()

    for src in alike:
        wait_fields(src)
        if groups > 1:
            passed_on(src).start()
    for slot in range(1, per_group):
        for to in others:
            vector_copy(to, slot).start()
        own_q(slot).start()
    own_f.wait()
    if groups > 1:
        wait_fields(mate)
        for src in alike:
            wait_fields(src + 1 - 2 * group)

    def unpack_fields(z):
        for which in range(2):
            rows = to_rows(
                [got_f[z, which, pl.ds(j, width, stride=FLAT)] for j in range(FLAT)]
            )
            for i in range(PACK):
                ab[which, z, i] = rows[i]

    for_planes(nz, unpack_fields)

    def beside(ref, part, z):
        rows = [ref[part, z + 1, i] for i in range(PACK)]
        above = jnp.where(not_first, pltpu.roll(rows[-1], 1, 0), 0.0)
        below = jnp.where(not_last, pltpu.roll(rows[0], width - 1, 0), 0.0)
        padded = [above] + rows + [below]
        sums = []
        for i in range(PACK):
            around = pltpu.roll(rows[i], 1, 1) + pltpu.roll(rows[i], LANES - 1, 1)
            around = around + (padded[i] + padded[i + 2])
            around = around + (ref[part, z, i] + ref[part, z + 2, i])
            sums.append(hop * around)
        return rows, sums

    def twice_operator(ref, z):
        u, near_u = beside(ref, 0, z)
        v, near_v = beside(ref, 1, z)
        results = []
        for i in range(PACK):
            a, b = ab[0, z, i], ab[1, z, i]
            results.append((a * u[i] + b * v[i] + near_u[i], b * u[i] - a * v[i] - near_v[i]))
        return results

    def clenshaw(now, then, scale, first=False):
        def plane(z):
            for i, pair in enumerate(twice_operator(now, z)):
                for part in range(2):
                    value = scale * q_rows[part, z, i] + pair[part]
                    if not first:
                        value = value - then[part, z + 1, i]
                    then[part, z + 1, i] = value

        for_planes(nz, plane)

    def sibling_copy(k):
        return pltpu.make_async_remote_copy(
            src_ref=dens.at[groups * k + 1 - group],
            dst_ref=sibling.at[k],
            send_sem=s_send.at[k],
            recv_sem=s_recv.at[k],
            device_id=(cut, mate),
            device_id_type=MESH,
        )

    def one_slot(slot, carry):
        own_q(slot).wait()
        for src in others:
            pltpu.make_async_remote_copy(
                src_ref=vectors.at[slot, pl.ds(own_start, width * FLAT)],
                dst_ref=got_q.at[slot, src],
                send_sem=q_send.at[slot, src],
                recv_sem=q_recv.at[slot, src],
                device_id=(cut, src),
                device_id_type=MESH,
            ).wait_recv()
        index = group * per_group + slot
        number = cut * cap + index
        level = slot_slice[number]
        weight = jnp.where(index < counts[cut], occupation[number], 0.0)
        last = coef[level, DEGREE]

        def unpack(z):
            for r in range(width * FLAT):
                wide[z, pl.ds(2 * r, 2)] = got_q[slot, z, r].astype(jnp.float32)
            for part in range(2):
                flat = [
                    wide[z, pl.ds(2 * j + part, width, stride=2 * FLAT)] for j in range(FLAT)
                ]
                rows = to_rows(flat)
                for i in range(PACK):
                    q_rows[part, z, i] = rows[i]
                    even[part, z + 1, i] = last * rows[i]

        for_planes(nz, unpack)
        clenshaw(even, odd, coef[level, DEGREE - 1], first=True)

        def two_steps(k, inner):
            order = DEGREE - 2 - 2 * k
            clenshaw(odd, even, coef[level, order])
            clenshaw(even, odd, coef[level, order - 1])
            return inner

        lax.fori_loop(0, (DEGREE - 2) // 2, two_steps, 0)
        base = coef[level, 0]

        def finish(z):
            for i, pair in enumerate(twice_operator(odd, z)):
                f = [
                    base * q_rows[part, z, i] + 0.5 * pair[part] - even[part, z + 1, i]
                    for part in range(2)
                ]
                heavy = weight * f[1]
                dens[z, 0, i] += heavy * f[1]
                dens[z, 1, i] += heavy * f[0]

        if groups == 1:
            for_planes(nz, finish)
            return carry
        for k in range(kept):
            finish(groups * k + 1 - group)
            pl.when(slot == per_group - 1)(sibling_copy(k).start)
        for k in range(kept):
            finish(groups * k + group)
        return carry

    lax.fori_loop(0, per_group, one_slot, 0)

    inside = piece * core - window * SUBLANES
    def part_copy(c, k):
        return pltpu.make_async_remote_copy(
            src_ref=parts.at[c, k],
            dst_ref=landed.at[cut],
            send_sem=p_send.at[c, k],
            recv_sem=p_recv.at[cut],
            device_id=(piece * near + c, groups * k + group),
            device_id_type=MESH,
        )

    def elsewhere(c, k):
        return jnp.logical_or(piece * near + c != cut, groups * k + group != slab)

    def pack(c, k):
        z = groups * k + group
        if share_rows % PACK == 0:
            step = share_rows // PACK
            spans = [(i, i, c * step, step) for i in range(PACK)]
        else:
            rows = [(r, c * share_rows + r) for r in range(share_rows)]
            spans = [(r, y % PACK, y // PACK, 1) for r, y in rows]
        for which in range(2):
            for r, i, g, n in spans:
                value = dens[z, which, i, pl.ds(inside + g, n)]
                if groups > 1:
                    value = value + sibling[k, which, i, pl.ds(inside + g, n)]
                if n == 1:
                    parts[c, k, pl.ds(which * share_rows + r, 1)] = value
                else:
                    parts[c, k, pl.ds(which * share_rows + r, n, stride=PACK)] = value

    for k in range(kept):
        if groups > 1:
            sibling_copy(k).wait_recv()
        for c in range(near):
            pack(c, k)
            pl.when(elsewhere(c, k))(part_copy(c, k).start)

    @pl.when(home == piece)
    def _():
        landed[cut] = parts[cut % near, slab // groups]

    for to in direct:
        field_copy(to).wait_send()
    if groups > 1:
        for src in alike:
            passed_on(src).wait_send()
    for to in others:
        for slot in range(per_group):
            vector_copy(to, slot).wait_send()
    for o in range(n_cuts):
        c = (cut + o) % n_cuts

        def arrive(c=c):
            pltpu.make_async_remote_copy(
                src_ref=parts.at[0, 0],
                dst_ref=landed.at[c],
                send_sem=p_send.at[0, 0],
                recv_sem=p_recv.at[c],
                device_id=(c, source_slab(c)),
                device_id_type=MESH,
            ).wait_recv()

        if o:
            arrive()
        else:
            pl.when(source_slab(c) != slab)(arrive)
    half = n_cuts // 2
    for i, some in enumerate((range(half), range(half, n_cuts))):
        total = jnp.zeros(landed.shape[1:], jnp.float32)
        for source in some:
            total = total + landed[source]
        out[i, pl.ds(0, 2 * share_rows)] = total[: 2 * share_rows]

    for k in range(kept):
        if groups > 1:
            sibling_copy(k).wait_send()
        for c in range(near):
            pl.when(elsewhere(c, k))(part_copy(c, k).wait_send)


def body(
    quasi, counts, slot_slice, occupation, filter_coef, trap_index, trap_table, mean_field, pairing
):
    n_cuts, nz = lax.axis_size("cuts"), lax.axis_size("slab")
    cap, flat = quasi.shape[1], quasi.shape[3]
    share = flat // n_cuts
    share_rows = share // NX
    groups, pieces, core, width, windows = plan(n_cuts, nz, cap, flat)
    per_group = cap // groups
    vectors = quasi.reshape(2, cap, flat // LANES, LANES).transpose(1, 2, 0, 3)

    rows = round_up(2 * share_rows, SUBLANES)
    near = n_cuts // pieces
    kept = nz // groups
    dims = (n_cuts, nz, groups, pieces, core, width, windows, per_group, share_rows)
    f32, i32 = jnp.float32, jnp.int32
    tall = (flat // LANES, LANES)
    slots = slot_slice.shape[0]
    sums = pl.pallas_call(
        functools.partial(kernel, dims),
        out_shape=jax.ShapeDtypeStruct((2, 3 * share_rows, LANES), f32),
        in_specs=[pl.BlockSpec(memory_space=pltpu.HBM)] * 8
        + [pl.BlockSpec(memory_space=pl.ANY)],
        out_specs=pl.BlockSpec(memory_space=pltpu.VMEM),
        scratch_shapes=[
            pltpu.SMEM((n_cuts,), i32),
            pltpu.SMEM((slots,), i32),
            pltpu.SMEM((slots,), f32),
            pltpu.SMEM(filter_coef.shape, f32),
            pltpu.SMEM(trap_table.shape, f32),
            pltpu.VMEM(tall, i32),
            pltpu.VMEM(tall, f32),
            pltpu.VMEM(tall, f32),
            pltpu.VMEM((2, PACK, flat // (NX * PACK), LANES), f32),
            pltpu.VMEM((2, *tall), f32),
            pltpu.VMEM((per_group, nz, FLAT * width, 2, LANES), jnp.bfloat16),
            pltpu.VMEM((nz, 2, FLAT * width, LANES), f32),
            pltpu.VMEM((nz, 2 * FLAT * width, LANES), f32),
            pltpu.VMEM((2, nz, PACK, width, LANES), f32),
            pltpu.VMEM((2, nz, PACK, width, LANES), f32),
            pltpu.VMEM((2, nz + 2, PACK, width, LANES), f32),
            pltpu.VMEM((2, nz + 2, PACK, width, LANES), f32),
            pltpu.VMEM((nz, 2, PACK, width, LANES), f32),
            pltpu.VMEM((kept, 2, PACK, width, LANES), f32),
            pltpu.VMEM((near, kept, rows, LANES), f32),
            pltpu.VMEM((n_cuts, rows, LANES), f32),
            pltpu.SemaphoreType.DMA((8,)),
            pltpu.SemaphoreType.DMA((per_group, nz)),
            pltpu.SemaphoreType.DMA((per_group, nz)),
            pltpu.SemaphoreType.DMA((2 * nz,)),
            pltpu.SemaphoreType.DMA((nz,)),
            pltpu.SemaphoreType.DMA((kept,)),
            pltpu.SemaphoreType.DMA((kept,)),
            pltpu.SemaphoreType.DMA((near, kept)),
            pltpu.SemaphoreType.DMA((n_cuts,)),
        ],
        compiler_params=pltpu.CompilerParams(
            collective_id=0, has_side_effects=True, vmem_limit_bytes=VMEM_BYTES
        ),
    )(
        counts,
        slot_slice,
        occupation,
        filter_coef,
        trap_table,
        trap_index.reshape(tall),
        mean_field.reshape(tall),
        pairing.reshape(tall),
        vectors,
    )

    halves = sums[:, :, :NX].reshape(6, share)
    normal_density = halves[0:1] + halves[3:4]
    anomalous_density = halves[1:2] + halves[4:5]
    mean_local, pairing_local = halves[2:3], halves[5:6]
    cube_root = jnp.cbrt(normal_density + density_floor)
    new_mean_field = 0.5 * mean_local + 0.5 * (beta_coef * cube_root * cube_root - chem_level)
    new_pairing = 0.5 * pairing_local - coupling * anomalous_density
    return (normal_density, anomalous_density, new_mean_field, new_pairing)


def solution(mesh):
    return jax.shard_map(
        body,
        mesh=mesh,
        in_specs=(
            P(None, "cuts", "slab", None),
            P(),
            P(),
            P(),
            P(),
            P("slab", None),
            P(),
            P("slab", None),
            P("slab", None),
        ),
        out_specs=(P("slab", "cuts"), P("slab", "cuts"), P("slab", "cuts"), P("slab", "cuts")),
        check_vma=False,
    )
```

```python
import functools

import jax
import jax.numpy as jnp
from jax import lax
from jax.experimental import pallas as pl
from jax.experimental.pallas import tpu as pltpu
from jax.sharding import PartitionSpec as P

NX = 96
DEGREE = 8
LANES = 128
PACK = 4
FLAT = 3
TILE = 16
SUBLANES = 8
VMEM_BYTES = 65000 * 1024

spectral_scale = 8.5
beta_coef = 0.6
chem_level = 1.0
coupling = 1.0
density_floor = 0.05

MESH = pl.DeviceIdType.MESH


def quotient(value, by):
    return lax.div(value, jnp.int32(by))


def modulo(value, by):
    return lax.rem(value, jnp.int32(by))


def round_up(value, step):
    return -(-value // step) * step


def plan(n_cuts, n_slab, cap, flat):
    groups = 2 if cap % 2 == 0 and n_slab % 2 == 0 else 1
    pieces = n_slab // groups
    total = flat // (NX * PACK)
    core = total // pieces
    halo = -(-DEGREE // PACK)
    width = min(round_up(core + halo, TILE), total)
    windows = (total - width) // SUBLANES + 1
    for piece in range(pieces):
        low, high = max(piece * core - halo, 0), min((piece + 1) * core + halo, total)
        start = SUBLANES * min(low // SUBLANES, windows - 1)
        assert start <= low and high <= start + width
    return groups, pieces, core, width, windows


def for_planes(count, body):
    chunk = 4 if count % 4 == 0 else 1
    if count == chunk:
        for z in range(chunk):
            body(z)
        return

    def some(i, carry):
        for z in range(chunk):
            body(i * chunk + z)
        return carry

    lax.fori_loop(0, count // chunk, some, 0)


def to_rows(flat_rows):
    p0, p1, p2 = flat_rows
    lane = lax.broadcasted_iota(jnp.int32, p0.shape, 1)
    r0, r1 = pltpu.roll(p0, 32, 1), pltpu.roll(p1, 32, 1)
    s1, s2 = pltpu.roll(p1, 64, 1), pltpu.roll(p2, 64, 1)
    rows = [
        p0,
        jnp.where(lane < 32, r0, r1),
        jnp.where(lane < 64, s1, s2),
        pltpu.roll(p2, 96, 1),
    ]
    return [jnp.where(lane < NX, row, 0.0) for row in rows]


def kernel(
    dims,
    counts_in,
    slot_slice_in,
    occupation_in,
    coef_in,
    table_in,
    index_in,
    mean_in,
    pairing_in,
    vectors,
    out,
    counts,
    slot_slice,
    occupation,
    coef,
    table,
    index_here,
    mean_here,
    pairing_here,
    local_rows,
    fields,
    got_q,
    got_f,
    wide,
    q_rows,
    ab,
    even,
    odd,
    dens,
    sibling,
    parts,
    landed,
    load_sem,
    q_send,
    q_recv,
    f_send,
    f_recv,
    s_send,
    s_recv,
    p_send,
    p_recv,
):
    n_cuts, nz, groups, pieces, core, width, windows, per_group, share_rows = dims
    cut, slab = lax.axis_index("cuts"), lax.axis_index("slab")
    near = n_cuts // pieces
    turn = max(near // 2, 1)
    home = quotient(cut, near)
    cap = per_group * groups
    kept = nz // groups
    halo = -(-DEGREE // PACK)

    def piece_of(s):
        return modulo(quotient(s, groups) + quotient(cut, turn), pieces)

    def window_of(p):
        low = jnp.maximum(p * core - halo, 0)
        return jnp.minimum(quotient(low, SUBLANES), windows - 1)

    piece, group = piece_of(slab), modulo(slab, groups)
    keeps_own = (home == piece).astype(jnp.int32)

    others = [modulo(slab + o, nz) for o in range(1, nz)]
    barrier = pltpu.get_barrier_semaphore()
    for to in others:
        pl.semaphore_signal(barrier, inc=1, device_id=(cut, to), device_id_type=MESH)

    loads = [
        pltpu.make_async_copy(src, dst, load_sem.at[i])
        for i, (src, dst) in enumerate(
            [
                (index_in, index_here),
                (table_in, table),
                (mean_in, mean_here),
                (pairing_in, pairing_here),
                (counts_in, counts),
                (slot_slice_in, slot_slice),
                (occupation_in, occupation),
                (coef_in, coef),
            ]
        )
    ]
    for load in loads[:4]:
        load.start()

    def source_slab(c):
        return modulo(home + pieces * n_cuts - quotient(c, turn), pieces) * groups + group

    for o in range(n_cuts):
        c = modulo(cut + o, n_cuts)
        s = source_slab(c)

        def greet(c=c, s=s):
            pl.semaphore_signal(barrier, inc=1, device_id=(c, s), device_id_type=MESH)

        if o:
            greet()
        else:
            pl.when(s != slab)(greet)

    for load in loads[:4]:
        load.wait()
    hits = index_here[...]
    trap = jnp.zeros(hits.shape, jnp.float32)
    for level in range(table.shape[0]):
        trap = jnp.where(hits == level, table[level], trap)
    fields[0] = (2.0 / spectral_scale) * (3.0 + (trap + mean_here[...]))
    fields[1] = (2.0 / spectral_scale) * pairing_here[...]

    pl.semaphore_wait(barrier, nz - 1 + near * kept - keeps_own)

    mate = slab + 1 - 2 * group

    def passed_on(src):
        return pltpu.make_async_remote_copy(
            src_ref=got_f.at[src],
            dst_ref=got_f.at[src],
            send_sem=f_send.at[nz + src],
            recv_sem=f_recv.at[src],
            device_id=(cut, mate),
            device_id_type=MESH,
        )

    def field_copy(to):
        start = pl.multiple_of(window_of(piece_of(to)) * (SUBLANES * FLAT), SUBLANES)
        return pltpu.make_async_remote_copy(
            src_ref=fields.at[:, pl.ds(start, width * FLAT)],
            dst_ref=got_f.at[slab],
            send_sem=f_send.at[to],
            recv_sem=f_recv.at[slab],
            device_id=(cut, to),
            device_id_type=MESH,
        )

    def vector_copy(to, slot):
        start = window_of(piece_of(to)) * (SUBLANES * FLAT)
        return pltpu.make_async_remote_copy(
            src_ref=vectors.at[modulo(to, groups) * per_group + slot, pl.ds(start, width * FLAT)],
            dst_ref=got_q.at[slot, slab],
            send_sem=q_send.at[slot, to],
            recv_sem=q_recv.at[slot, slab],
            device_id=(cut, to),
            device_id_type=MESH,
        )

    window = window_of(piece)
    alike = [modulo(slab + o, nz) for o in range(groups, nz, groups)]
    direct = alike + ([mate] if groups > 1 else [])
    for to in direct:
        field_copy(to).start()
    for to in others:
        vector_copy(to, 0).start()
    own_start = pl.multiple_of(window * (SUBLANES * FLAT), SUBLANES)
    own_f = pltpu.make_async_copy(
        fields.at[:, pl.ds(own_start, width * FLAT)], got_f.at[slab], f_recv.at[slab]
    )
    own_f.start()

    def own_q(slot):
        return pltpu.make_async_copy(
            vectors.at[group * per_group + slot, pl.ds(own_start, width * FLAT)],
            got_q.at[slot, slab],
            q_recv.at[slot, slab],
        )

    own_q(0).start()
    for slot in range(1, per_group):
        for to in others:
            vector_copy(to, slot).start()
        own_q(slot).start()
    for load in loads[4:]:
        load.start()

    lane = lax.broadcasted_iota(jnp.int32, (width, LANES), 1)
    line = lax.broadcasted_iota(jnp.int32, (width, LANES), 0)
    not_first, not_last = line > 0, line < width - 1
    hop = jnp.where(lane < NX, -1.0 / spectral_scale, 0.0).astype(jnp.float32)

    blank = jnp.zeros((2, PACK, width, LANES), jnp.float32)
    for buffer in (even, odd):
        buffer[:, 0] = blank
        buffer[:, nz + 1] = blank
    dens[...] = jnp.zeros(dens.shape, jnp.float32)

    def wait_fields(src):
        pltpu.make_async_remote_copy(
            src_ref=fields.at[:, pl.ds(own_start, width * FLAT)],
            dst_ref=got_f.at[src],
            send_sem=f_send.at[src],
            recv_sem=f_recv.at[src],
            device_id=(cut, src),
            device_id_type=MESH,
        ).wait_recv()

    for src in alike:
        wait_fields(src)
        if groups > 1:
            passed_on(src).start()
    own_f.wait()
    if groups > 1:
        wait_fields(mate)
        for src in alike:
            wait_fields(src + 1 - 2 * group)

    for load in loads[4:]:
        load.wait()

    def unpack_fields(z):
        for which in range(2):
            rows = to_rows(
                [got_f[z, which, pl.ds(j, width, stride=FLAT)] for j in range(FLAT)]
            )
            for i in range(PACK):
                ab[which, z, i] = rows[i]

    for_planes(nz, unpack_fields)

    def beside(ref, part, z):
        rows = [ref[part, z + 1, i] for i in range(PACK)]
        above = jnp.where(not_first, pltpu.roll(rows[-1], 1, 0), 0.0)
        below = jnp.where(not_last, pltpu.roll(rows[0], width - 1, 0), 0.0)
        padded = [above] + rows + [below]
        sums = []
        for i in range(PACK):
            around = pltpu.roll(rows[i], 1, 1) + pltpu.roll(rows[i], LANES - 1, 1)
            around = around + (padded[i] + padded[i + 2])
            around = around + (ref[part, z, i] + ref[part, z + 2, i])
            sums.append(hop * around)
        return rows, sums

    def twice_operator(ref, z):
        u, near_u = beside(ref, 0, z)
        v, near_v = beside(ref, 1, z)
        results = []
        for i in range(PACK):
            a, b = ab[0, z, i], ab[1, z, i]
            results.append((a * u[i] + b * v[i] + near_u[i], b * u[i] - a * v[i] - near_v[i]))
        return results

    def clenshaw(now, then, scale, first=False):
        def plane(z):
            for i, pair in enumerate(twice_operator(now, z)):
                for part in range(2):
                    value = scale * q_rows[part, z, i] + pair[part]
                    if not first:
                        value = value - then[part, z + 1, i]
                    then[part, z + 1, i] = value

        for_planes(nz, plane)

    def sibling_copy(k):
        return pltpu.make_async_remote_copy(
            src_ref=dens.at[groups * k + 1 - group],
            dst_ref=sibling.at[k],
            send_sem=s_send.at[k],
            recv_sem=s_recv.at[k],
            device_id=(cut, mate),
            device_id_type=MESH,
        )

    def one_slot(slot, carry):
        own_q(slot).wait()
        for src in others:
            pltpu.make_async_remote_copy(
                src_ref=vectors.at[slot, pl.ds(own_start, width * FLAT)],
                dst_ref=got_q.at[slot, src],
                send_sem=q_send.at[slot, src],
                recv_sem=q_recv.at[slot, src],
                device_id=(cut, src),
                device_id_type=MESH,
            ).wait_recv()
        index = group * per_group + slot
        number = cut * cap + index
        level = slot_slice[number]
        weight = jnp.where(index < counts[cut], occupation[number], 0.0)
        last = coef[level, DEGREE]

        def unpack(z):
            for r in range(width * FLAT):
                wide[z, pl.ds(2 * r, 2)] = got_q[slot, z, r].astype(jnp.float32)
            for part in range(2):
                flat = [
                    wide[z, pl.ds(2 * j + part, width, stride=2 * FLAT)] for j in range(FLAT)
                ]
                rows = to_rows(flat)
                for i in range(PACK):
                    q_rows[part, z, i] = rows[i]
                    even[part, z + 1, i] = last * rows[i]

        for_planes(nz, unpack)
        clenshaw(even, odd, coef[level, DEGREE - 1], first=True)

        def two_steps(k, inner):
            order = DEGREE - 2 - 2 * k
            clenshaw(odd, even, coef[level, order])
            clenshaw(even, odd, coef[level, order - 1])
            return inner

        lax.fori_loop(0, (DEGREE - 2) // 2, two_steps, 0)
        base = coef[level, 0]

        def finish(z):
            for i, pair in enumerate(twice_operator(odd, z)):
                f = [
                    base * q_rows[part, z, i] + 0.5 * pair[part] - even[part, z + 1, i]
                    for part in range(2)
                ]
                heavy = weight * f[1]
                dens[z, 0, i] += heavy * f[1]
                dens[z, 1, i] += heavy * f[0]

        if groups == 1:
            for_planes(nz, finish)
            return carry
        for k in range(kept):
            finish(groups * k + 1 - group)
            pl.when(slot == per_group - 1)(sibling_copy(k).start)
        for k in range(kept):
            finish(groups * k + group)
        return carry

    lax.fori_loop(0, per_group, one_slot, 0)

    inside = piece * core - window * SUBLANES
    def part_copy(c, k):
        return pltpu.make_async_remote_copy(
            src_ref=parts.at[c, k],
            dst_ref=landed.at[cut],
            send_sem=p_send.at[c, k],
            recv_sem=p_recv.at[cut],
            device_id=(piece * near + c, groups * k + group),
            device_id_type=MESH,
        )

    def elsewhere(c, k):
        return jnp.logical_or(piece * near + c != cut, groups * k + group != slab)

    def pack(c, k):
        z = groups * k + group
        if share_rows % PACK == 0:
            step = share_rows // PACK
            spans = [(i, i, c * step, step) for i in range(PACK)]
        else:
            rows = [(r, c * share_rows + r) for r in range(share_rows)]
            spans = [(r, y % PACK, y // PACK, 1) for r, y in rows]
        for which in range(2):
            for r, i, g, n in spans:
                value = dens[z, which, i, pl.ds(inside + g, n)]
                if groups > 1:
                    value = value + sibling[k, which, i, pl.ds(inside + g, n)]
                if n == 1:
                    parts[c, k, pl.ds(which * share_rows + r, 1)] = value
                else:
                    parts[c, k, pl.ds(which * share_rows + r, n, stride=PACK)] = value

    for k in range(kept):
        if groups > 1:
            sibling_copy(k).wait_recv()
        for c in range(near):
            pack(c, k)
            pl.when(elsewhere(c, k))(part_copy(c, k).start)

    @pl.when(home == piece)
    def _():
        landed[cut] = parts[modulo(cut, near), quotient(slab, groups)]

    for part, here in enumerate((mean_here, pairing_here)):
        count = here.shape[0] // FLAT
        rows = to_rows([here[pl.ds(j, count, stride=FLAT)] for j in range(FLAT)])
        for i in range(PACK):
            local_rows[part, i] = rows[i]
        for r in range(share_rows):
            y = cut * share_rows + r
            out[part, pl.ds(2 * share_rows + r, 1)] = local_rows[
                part, modulo(y, PACK), pl.ds(quotient(y, PACK), 1)
            ]

    for to in direct:
        field_copy(to).wait_send()
    if groups > 1:
        for src in alike:
            passed_on(src).wait_send()
    for to in others:
        for slot in range(per_group):
            vector_copy(to, slot).wait_send()
    for o in range(n_cuts):
        c = modulo(cut + o, n_cuts)

        def arrive(c=c):
            pltpu.make_async_remote_copy(
                src_ref=parts.at[0, 0],
                dst_ref=landed.at[c],
                send_sem=p_send.at[0, 0],
                recv_sem=p_recv.at[c],
                device_id=(c, source_slab(c)),
                device_id_type=MESH,
            ).wait_recv()

        if o:
            arrive()
        else:
            pl.when(source_slab(c) != slab)(arrive)
    half = n_cuts // 2
    for i, some in enumerate((range(half), range(half, n_cuts))):
        total = jnp.zeros(landed.shape[1:], jnp.float32)
        for source in some:
            total = total + landed[source]
        out[i, pl.ds(0, 2 * share_rows)] = total[: 2 * share_rows]

    for k in range(kept):
        if groups > 1:
            sibling_copy(k).wait_send()
        for c in range(near):
            pl.when(elsewhere(c, k))(part_copy(c, k).wait_send)


def body(
    quasi, counts, slot_slice, occupation, filter_coef, trap_index, trap_table, mean_field, pairing
):
    n_cuts, nz = lax.axis_size("cuts"), lax.axis_size("slab")
    cap, flat = quasi.shape[1], quasi.shape[3]
    share = flat // n_cuts
    share_rows = share // NX
    groups, pieces, core, width, windows = plan(n_cuts, nz, cap, flat)
    per_group = cap // groups
    vectors = quasi.reshape(2, cap, flat // LANES, LANES).transpose(1, 2, 0, 3)

    rows = round_up(2 * share_rows, SUBLANES)
    near = n_cuts // pieces
    kept = nz // groups
    dims = (n_cuts, nz, groups, pieces, core, width, windows, per_group, share_rows)
    f32, i32 = jnp.float32, jnp.int32
    tall = (flat // LANES, LANES)
    slots = slot_slice.shape[0]
    sums = pl.pallas_call(
        functools.partial(kernel, dims),
        out_shape=jax.ShapeDtypeStruct((2, 3 * share_rows, LANES), f32),
        in_specs=[pl.BlockSpec(memory_space=pltpu.HBM)] * 8
        + [pl.BlockSpec(memory_space=pl.ANY)],
        out_specs=pl.BlockSpec(memory_space=pltpu.VMEM),
        scratch_shapes=[
            pltpu.SMEM((n_cuts,), i32),
            pltpu.SMEM((slots,), i32),
            pltpu.SMEM((slots,), f32),
            pltpu.SMEM(filter_coef.shape, f32),
            pltpu.SMEM(trap_table.shape, f32),
            pltpu.VMEM(tall, i32),
            pltpu.VMEM(tall, f32),
            pltpu.VMEM(tall, f32),
            pltpu.VMEM((2, PACK, flat // (NX * PACK), LANES), f32),
            pltpu.VMEM((2, *tall), f32),
            pltpu.VMEM((per_group, nz, FLAT * width, 2, LANES), jnp.bfloat16),
            pltpu.VMEM((nz, 2, FLAT * width, LANES), f32),
            pltpu.VMEM((nz, 2 * FLAT * width, LANES), f32),
            pltpu.VMEM((2, nz, PACK, width, LANES), f32),
            pltpu.VMEM((2, nz, PACK, width, LANES), f32),
            pltpu.VMEM((2, nz + 2, PACK, width, LANES), f32),
            pltpu.VMEM((2, nz + 2, PACK, width, LANES), f32),
            pltpu.VMEM((nz, 2, PACK, width, LANES), f32),
            pltpu.VMEM((kept, 2, PACK, width, LANES), f32),
            pltpu.VMEM((near, kept, rows, LANES), f32),
            pltpu.VMEM((n_cuts, rows, LANES), f32),
            pltpu.SemaphoreType.DMA((8,)),
            pltpu.SemaphoreType.DMA((per_group, nz)),
            pltpu.SemaphoreType.DMA((per_group, nz)),
            pltpu.SemaphoreType.DMA((2 * nz,)),
            pltpu.SemaphoreType.DMA((nz,)),
            pltpu.SemaphoreType.DMA((kept,)),
            pltpu.SemaphoreType.DMA((kept,)),
            pltpu.SemaphoreType.DMA((near, kept)),
            pltpu.SemaphoreType.DMA((n_cuts,)),
        ],
        compiler_params=pltpu.CompilerParams(
            collective_id=0, has_side_effects=True, vmem_limit_bytes=VMEM_BYTES
        ),
    )(
        counts,
        slot_slice,
        occupation,
        filter_coef,
        trap_table,
        trap_index.reshape(tall),
        mean_field.reshape(tall),
        pairing.reshape(tall),
        vectors,
    )

    halves = sums[:, :, :NX].reshape(6, share)
    normal_density = halves[0:1] + halves[3:4]
    anomalous_density = halves[1:2] + halves[4:5]
    mean_local, pairing_local = halves[2:3], halves[5:6]
    cube_root = jnp.cbrt(normal_density + density_floor)
    new_mean_field = 0.5 * mean_local + 0.5 * (beta_coef * cube_root * cube_root - chem_level)
    new_pairing = 0.5 * pairing_local - coupling * anomalous_density
    return (normal_density, anomalous_density, new_mean_field, new_pairing)


def solution(mesh):
    return jax.shard_map(
        body,
        mesh=mesh,
        in_specs=(
            P(None, "cuts", "slab", None),
            P(),
            P(),
            P(),
            P(),
            P("slab", None),
            P(),
            P("slab", None),
            P("slab", None),
        ),
        out_specs=(P("slab", "cuts"), P("slab", "cuts"), P("slab", "cuts"), P("slab", "cuts")),
        check_vma=False,
    )
```

```python
import functools

import jax
import jax.numpy as jnp
from jax import lax
from jax.experimental import pallas as pl
from jax.experimental.pallas import tpu as pltpu
from jax.sharding import PartitionSpec as P

NX = 96
DEGREE = 8
LANES = 128
PACK = 4
FLAT = 3
TILE = 16
SUBLANES = 8
VMEM_BYTES = 65000 * 1024

spectral_scale = 8.5
beta_coef = 0.6
chem_level = 1.0
coupling = 1.0
density_floor = 0.05

MESH = pl.DeviceIdType.MESH


def quotient(value, by):
    return lax.div(value, jnp.int32(by))


def modulo(value, by):
    return lax.rem(value, jnp.int32(by))


def round_up(value, step):
    return -(-value // step) * step


def plan(n_cuts, n_slab, cap, flat):
    groups = 2 if cap % 2 == 0 and n_slab % 2 == 0 else 1
    pieces = n_slab // groups
    total = flat // (NX * PACK)
    core = total // pieces
    halo = -(-DEGREE // PACK)
    width = min(round_up(core + halo, TILE), total)
    windows = (total - width) // SUBLANES + 1
    for piece in range(pieces):
        low, high = max(piece * core - halo, 0), min((piece + 1) * core + halo, total)
        start = SUBLANES * min(low // SUBLANES, windows - 1)
        assert start <= low and high <= start + width
    return groups, pieces, core, width, windows


def for_planes(count, body):
    chunk = 4 if count % 4 == 0 else 1
    if count == chunk:
        for z in range(chunk):
            body(z)
        return

    def some(i, carry):
        for z in range(chunk):
            body(i * chunk + z)
        return carry

    lax.fori_loop(0, count // chunk, some, 0)


def to_rows(flat_rows):
    p0, p1, p2 = flat_rows
    lane = lax.broadcasted_iota(jnp.int32, p0.shape, 1)
    r0, r1 = pltpu.roll(p0, 32, 1), pltpu.roll(p1, 32, 1)
    s1, s2 = pltpu.roll(p1, 64, 1), pltpu.roll(p2, 64, 1)
    rows = [
        p0,
        jnp.where(lane < 32, r0, r1),
        jnp.where(lane < 64, s1, s2),
        pltpu.roll(p2, 96, 1),
    ]
    return [jnp.where(lane < NX, row, 0.0) for row in rows]


def kernel(
    dims,
    counts_in,
    slot_slice_in,
    occupation_in,
    coef_in,
    table_in,
    index_in,
    mean_in,
    pairing_in,
    vectors,
    out,
    counts,
    slot_slice,
    occupation,
    coef,
    table,
    index_here,
    mean_here,
    pairing_here,
    local_rows,
    fields,
    got_q,
    got_f,
    wide,
    q_rows,
    ab,
    even,
    odd,
    dens,
    sibling,
    parts,
    landed,
    load_sem,
    q_send,
    q_recv,
    f_send,
    f_recv,
    s_send,
    s_recv,
    p_send,
    p_recv,
):
    n_cuts, nz, groups, pieces, core, width, windows, per_group, share_rows = dims
    cut, slab = lax.axis_index("cuts"), lax.axis_index("slab")
    near = n_cuts // pieces
    turn = max(near // 2, 1)
    home = quotient(cut, near)
    cap = per_group * groups
    kept = nz // groups
    halo = -(-DEGREE // PACK)

    def piece_of(s):
        return modulo(quotient(s, groups) + quotient(cut, turn), pieces)

    def window_of(p):
        low = jnp.maximum(p * core - halo, 0)
        return jnp.minimum(quotient(low, SUBLANES), windows - 1)

    piece, group = piece_of(slab), modulo(slab, groups)
    keeps_own = (home == piece).astype(jnp.int32)

    others = [modulo(slab + o, nz) for o in range(1, nz)]
    barrier = pltpu.get_barrier_semaphore()
    for to in others:
        pl.semaphore_signal(barrier, inc=1, device_id=(cut, to), device_id_type=MESH)

    loads = [
        pltpu.make_async_copy(src, dst, load_sem.at[i])
        for i, (src, dst) in enumerate(
            [
                (index_in, index_here),
                (table_in, table),
                (mean_in, mean_here),
                (pairing_in, pairing_here),
                (counts_in, counts),
                (slot_slice_in, slot_slice),
                (occupation_in, occupation),
                (coef_in, coef),
            ]
        )
    ]
    for load in loads[:4]:
        load.start()

    def source_slab(c):
        return modulo(home + pieces * n_cuts - quotient(c, turn), pieces) * groups + group

    for o in range(n_cuts):
        c = modulo(cut + o, n_cuts)
        s = source_slab(c)

        def greet(c=c, s=s):
            pl.semaphore_signal(barrier, inc=1, device_id=(c, s), device_id_type=MESH)

        if o:
            greet()
        else:
            pl.when(s != slab)(greet)

    for load in loads[:4]:
        load.wait()
    hits = index_here[...]
    trap = jnp.zeros(hits.shape, jnp.float32)
    for level in range(table.shape[0]):
        trap = jnp.where(hits == level, table[level], trap)
    fields[0] = (2.0 / spectral_scale) * (3.0 + (trap + mean_here[...]))
    fields[1] = (2.0 / spectral_scale) * pairing_here[...]

    pl.semaphore_wait(barrier, nz - 1 + near * kept - keeps_own)

    mate = slab + 1 - 2 * group

    def passed_on(src):
        return pltpu.make_async_remote_copy(
            src_ref=got_f.at[src],
            dst_ref=got_f.at[src],
            send_sem=f_send.at[nz + src],
            recv_sem=f_recv.at[src],
            device_id=(cut, mate),
            device_id_type=MESH,
        )

    def field_copy(to):
        start = pl.multiple_of(window_of(piece_of(to)) * (SUBLANES * FLAT), SUBLANES)
        return pltpu.make_async_remote_copy(
            src_ref=fields.at[:, pl.ds(start, width * FLAT)],
            dst_ref=got_f.at[slab],
            send_sem=f_send.at[to],
            recv_sem=f_recv.at[slab],
            device_id=(cut, to),
            device_id_type=MESH,
        )

    def vector_copy(to, slot):
        start = window_of(piece_of(to)) * (SUBLANES * FLAT)
        return pltpu.make_async_remote_copy(
            src_ref=vectors.at[modulo(to, groups) * per_group + slot, pl.ds(start, width * FLAT)],
            dst_ref=got_q.at[slot, slab],
            send_sem=q_send.at[slot, to],
            recv_sem=q_recv.at[slot, slab],
            device_id=(cut, to),
            device_id_type=MESH,
        )

    window = window_of(piece)
    alike = [modulo(slab + o, nz) for o in range(groups, nz, groups)]
    direct = alike + ([mate] if groups > 1 else [])
    for to in direct:
        field_copy(to).start()
    for to in others:
        vector_copy(to, 0).start()
    own_start = pl.multiple_of(window * (SUBLANES * FLAT), SUBLANES)
    own_f = pltpu.make_async_copy(
        fields.at[:, pl.ds(own_start, width * FLAT)], got_f.at[slab], f_recv.at[slab]
    )
    own_f.start()

    def own_q(slot):
        return pltpu.make_async_copy(
            vectors.at[group * per_group + slot, pl.ds(own_start, width * FLAT)],
            got_q.at[slot, slab],
            q_recv.at[slot, slab],
        )

    own_q(0).start()
    for slot in range(1, per_group):
        for to in others:
            vector_copy(to, slot).start()
        own_q(slot).start()
    for load in loads[4:]:
        load.start()

    lane = lax.broadcasted_iota(jnp.int32, (width, LANES), 1)
    line = lax.broadcasted_iota(jnp.int32, (width, LANES), 0)
    not_first, not_last = line > 0, line < width - 1
    hop = jnp.where(lane < NX, -1.0 / spectral_scale, 0.0).astype(jnp.float32)

    blank = jnp.zeros((2, PACK, width, LANES), jnp.float32)
    for buffer in (even, odd):
        buffer[:, 0] = blank
        buffer[:, nz + 1] = blank
    dens[...] = jnp.zeros(dens.shape, jnp.float32)

    def wait_fields(src):
        pltpu.make_async_remote_copy(
            src_ref=fields.at[:, pl.ds(own_start, width * FLAT)],
            dst_ref=got_f.at[src],
            send_sem=f_send.at[src],
            recv_sem=f_recv.at[src],
            device_id=(cut, src),
            device_id_type=MESH,
        ).wait_recv()

    for src in alike:
        wait_fields(src)
        if groups > 1:
            passed_on(src).start()
    own_f.wait()
    if groups > 1:
        wait_fields(mate)
        for src in alike:
            wait_fields(src + 1 - 2 * group)

    for load in loads[4:]:
        load.wait()

    def unpack_fields(z):
        for which in range(2):
            rows = to_rows(
                [got_f[z, which, pl.ds(j, width, stride=FLAT)] for j in range(FLAT)]
            )
            for i in range(PACK):
                ab[which, z, i] = rows[i]

    for_planes(nz, unpack_fields)

    def beside(ref, part, z):
        rows = [ref[part, z + 1, i] for i in range(PACK)]
        above = jnp.where(not_first, pltpu.roll(rows[-1], 1, 0), 0.0)
        below = jnp.where(not_last, pltpu.roll(rows[0], width - 1, 0), 0.0)
        padded = [above] + rows + [below]
        sums = []
        for i in range(PACK):
            around = pltpu.roll(rows[i], 1, 1) + pltpu.roll(rows[i], LANES - 1, 1)
            around = around + (padded[i] + padded[i + 2])
            if not (isinstance(z, int) and z == 0):
                around = around + ref[part, z, i]
            if not (isinstance(z, int) and z == nz - 1):
                around = around + ref[part, z + 2, i]
            sums.append(hop * around)
        return rows, sums

    def twice_operator(ref, z):
        u, near_u = beside(ref, 0, z)
        v, near_v = beside(ref, 1, z)
        results = []
        for i in range(PACK):
            a, b = ab[0, z, i], ab[1, z, i]
            results.append((a * u[i] + b * v[i] + near_u[i], b * u[i] - a * v[i] - near_v[i]))
        return results

    def clenshaw(now, then, scale, first=False):
        def plane(z):
            for i, pair in enumerate(twice_operator(now, z)):
                for part in range(2):
                    value = scale * q_rows[part, z, i] + pair[part]
                    if not first:
                        value = value - then[part, z + 1, i]
                    then[part, z + 1, i] = value

        for_planes(nz, plane)

    def sibling_copy(k):
        return pltpu.make_async_remote_copy(
            src_ref=dens.at[groups * k + 1 - group],
            dst_ref=sibling.at[k],
            send_sem=s_send.at[k],
            recv_sem=s_recv.at[k],
            device_id=(cut, mate),
            device_id_type=MESH,
        )

    def one_slot(slot, carry):
        own_q(slot).wait()
        for src in others:
            pltpu.make_async_remote_copy(
                src_ref=vectors.at[slot, pl.ds(own_start, width * FLAT)],
                dst_ref=got_q.at[slot, src],
                send_sem=q_send.at[slot, src],
                recv_sem=q_recv.at[slot, src],
                device_id=(cut, src),
                device_id_type=MESH,
            ).wait_recv()
        index = group * per_group + slot
        number = cut * cap + index
        level = slot_slice[number]
        weight = jnp.where(index < counts[cut], occupation[number], 0.0)
        last = coef[level, DEGREE]

        def unpack(z):
            for r in range(width * FLAT):
                wide[z, pl.ds(2 * r, 2)] = got_q[slot, z, r].astype(jnp.float32)
            for part in range(2):
                flat = [
                    wide[z, pl.ds(2 * j + part, width, stride=2 * FLAT)] for j in range(FLAT)
                ]
                rows = to_rows(flat)
                for i in range(PACK):
                    q_rows[part, z, i] = rows[i]
                    even[part, z + 1, i] = last * rows[i]

        for_planes(nz, unpack)
        clenshaw(even, odd, coef[level, DEGREE - 1], first=True)

        def two_steps(k, inner):
            order = DEGREE - 2 - 2 * k
            clenshaw(odd, even, coef[level, order])
            clenshaw(even, odd, coef[level, order - 1])
            return inner

        lax.fori_loop(0, (DEGREE - 2) // 2, two_steps, 0)
        base = coef[level, 0]

        def finish(z):
            for i, pair in enumerate(twice_operator(odd, z)):
                f = [
                    base * q_rows[part, z, i] + 0.5 * pair[part] - even[part, z + 1, i]
                    for part in range(2)
                ]
                heavy = weight * f[1]
                dens[z, 0, i] += heavy * f[1]
                dens[z, 1, i] += heavy * f[0]

        if groups == 1:
            for_planes(nz, finish)
            return carry
        for k in range(kept):
            finish(groups * k + 1 - group)
            pl.when(slot == per_group - 1)(sibling_copy(k).start)
        for k in range(kept):
            finish(groups * k + group)
        return carry

    lax.fori_loop(0, per_group, one_slot, 0)

    inside = piece * core - window * SUBLANES
    def part_copy(c, k):
        return pltpu.make_async_remote_copy(
            src_ref=parts.at[c, k],
            dst_ref=landed.at[cut],
            send_sem=p_send.at[c, k],
            recv_sem=p_recv.at[cut],
            device_id=(piece * near + c, groups * k + group),
            device_id_type=MESH,
        )

    def elsewhere(c, k):
        return jnp.logical_or(piece * near + c != cut, groups * k + group != slab)

    def pack(c, k):
        z = groups * k + group
        if share_rows % PACK == 0:
            step = share_rows // PACK
            spans = [(i, i, c * step, step) for i in range(PACK)]
        else:
            rows = [(r, c * share_rows + r) for r in range(share_rows)]
            spans = [(r, y % PACK, y // PACK, 1) for r, y in rows]
        for which in range(2):
            for r, i, g, n in spans:
                value = dens[z, which, i, pl.ds(inside + g, n)]
                if groups > 1:
                    value = value + sibling[k, which, i, pl.ds(inside + g, n)]
                if n == 1:
                    parts[c, k, pl.ds(which * share_rows + r, 1)] = value
                else:
                    parts[c, k, pl.ds(which * share_rows + r, n, stride=PACK)] = value

    for k in range(kept):
        if groups > 1:
            sibling_copy(k).wait_recv()
        for c in range(near):
            pack(c, k)
            pl.when(elsewhere(c, k))(part_copy(c, k).start)

    @pl.when(home == piece)
    def _():
        landed[cut] = parts[modulo(cut, near), quotient(slab, groups)]

    for part, here in enumerate((mean_here, pairing_here)):
        count = here.shape[0] // FLAT
        rows = to_rows([here[pl.ds(j, count, stride=FLAT)] for j in range(FLAT)])
        for i in range(PACK):
            local_rows[part, i] = rows[i]
        for r in range(share_rows):
            y = cut * share_rows + r
            out[part, pl.ds(2 * share_rows + r, 1)] = local_rows[
                part, modulo(y, PACK), pl.ds(quotient(y, PACK), 1)
            ]

    for to in direct:
        field_copy(to).wait_send()
    if groups > 1:
        for src in alike:
            passed_on(src).wait_send()
    for to in others:
        for slot in range(per_group):
            vector_copy(to, slot).wait_send()
    for o in range(n_cuts):
        c = modulo(cut + o, n_cuts)

        def arrive(c=c):
            pltpu.make_async_remote_copy(
                src_ref=parts.at[0, 0],
                dst_ref=landed.at[c],
                send_sem=p_send.at[0, 0],
                recv_sem=p_recv.at[c],
                device_id=(c, source_slab(c)),
                device_id_type=MESH,
            ).wait_recv()

        if o:
            arrive()
        else:
            pl.when(source_slab(c) != slab)(arrive)
    half = n_cuts // 2
    for i, some in enumerate((range(half), range(half, n_cuts))):
        total = jnp.zeros(landed.shape[1:], jnp.float32)
        for source in some:
            total = total + landed[source]
        out[i, pl.ds(0, 2 * share_rows)] = total[: 2 * share_rows]

    for k in range(kept):
        if groups > 1:
            sibling_copy(k).wait_send()
        for c in range(near):
            pl.when(elsewhere(c, k))(part_copy(c, k).wait_send)


def body(
    quasi, counts, slot_slice, occupation, filter_coef, trap_index, trap_table, mean_field, pairing
):
    n_cuts, nz = lax.axis_size("cuts"), lax.axis_size("slab")
    cap, flat = quasi.shape[1], quasi.shape[3]
    share = flat // n_cuts
    share_rows = share // NX
    groups, pieces, core, width, windows = plan(n_cuts, nz, cap, flat)
    per_group = cap // groups
    vectors = quasi.reshape(2, cap, flat // LANES, LANES).transpose(1, 2, 0, 3)

    rows = round_up(2 * share_rows, SUBLANES)
    near = n_cuts // pieces
    kept = nz // groups
    dims = (n_cuts, nz, groups, pieces, core, width, windows, per_group, share_rows)
    f32, i32 = jnp.float32, jnp.int32
    tall = (flat // LANES, LANES)
    slots = slot_slice.shape[0]
    sums = pl.pallas_call(
        functools.partial(kernel, dims),
        out_shape=pltpu.VMEM((2, 3 * share_rows, LANES), f32),
        in_specs=[pl.BlockSpec(memory_space=pltpu.HBM)] * 8
        + [pl.BlockSpec(memory_space=pl.ANY)],
        out_specs=pl.BlockSpec(memory_space=pltpu.VMEM),
        scratch_shapes=[
            pltpu.SMEM((n_cuts,), i32),
            pltpu.SMEM((slots,), i32),
            pltpu.SMEM((slots,), f32),
            pltpu.SMEM(filter_coef.shape, f32),
            pltpu.SMEM(trap_table.shape, f32),
            pltpu.VMEM(tall, i32),
            pltpu.VMEM(tall, f32),
            pltpu.VMEM(tall, f32),
            pltpu.VMEM((2, PACK, flat // (NX * PACK), LANES), f32),
            pltpu.VMEM((2, *tall), f32),
            pltpu.VMEM((per_group, nz, FLAT * width, 2, LANES), jnp.bfloat16),
            pltpu.VMEM((nz, 2, FLAT * width, LANES), f32),
            pltpu.VMEM((nz, 2 * FLAT * width, LANES), f32),
            pltpu.VMEM((2, nz, PACK, width, LANES), f32),
            pltpu.VMEM((2, nz, PACK, width, LANES), f32),
            pltpu.VMEM((2, nz + 2, PACK, width, LANES), f32),
            pltpu.VMEM((2, nz + 2, PACK, width, LANES), f32),
            pltpu.VMEM((nz, 2, PACK, width, LANES), f32),
            pltpu.VMEM((kept, 2, PACK, width, LANES), f32),
            pltpu.VMEM((near, kept, rows, LANES), f32),
            pltpu.VMEM((n_cuts, rows, LANES), f32),
            pltpu.SemaphoreType.DMA((8,)),
            pltpu.SemaphoreType.DMA((per_group, nz)),
            pltpu.SemaphoreType.DMA((per_group, nz)),
            pltpu.SemaphoreType.DMA((2 * nz,)),
            pltpu.SemaphoreType.DMA((nz,)),
            pltpu.SemaphoreType.DMA((kept,)),
            pltpu.SemaphoreType.DMA((kept,)),
            pltpu.SemaphoreType.DMA((near, kept)),
            pltpu.SemaphoreType.DMA((n_cuts,)),
        ],
        compiler_params=pltpu.CompilerParams(
            collective_id=0, has_side_effects=True, vmem_limit_bytes=VMEM_BYTES
        ),
    )(
        counts,
        slot_slice,
        occupation,
        filter_coef,
        trap_table,
        trap_index.reshape(tall),
        mean_field.reshape(tall),
        pairing.reshape(tall),
        vectors,
    )

    halves = sums[:, :, :NX].reshape(6, share)
    normal_density = halves[0:1] + halves[3:4]
    anomalous_density = halves[1:2] + halves[4:5]
    mean_local, pairing_local = halves[2:3], halves[5:6]
    cube_root = jnp.cbrt(normal_density + density_floor)
    new_mean_field = 0.5 * mean_local + 0.5 * (beta_coef * cube_root * cube_root - chem_level)
    new_pairing = 0.5 * pairing_local - coupling * anomalous_density
    return (normal_density, anomalous_density, new_mean_field, new_pairing)


def solution(mesh):
    return jax.shard_map(
        body,
        mesh=mesh,
        in_specs=(
            P(None, "cuts", "slab", None),
            P(),
            P(),
            P(),
            P(),
            P("slab", None),
            P(),
            P("slab", None),
            P("slab", None),
        ),
        out_specs=(P("slab", "cuts"), P("slab", "cuts"), P("slab", "cuts"), P("slab", "cuts")),
        check_vma=False,
    )
```

```python
import functools

import jax
import jax.numpy as jnp
from jax import lax
from jax.experimental import pallas as pl
from jax.experimental.pallas import tpu as pltpu
from jax.sharding import PartitionSpec as P

NX = 96
DEGREE = 8
LANES = 128
PACK = 4
FLAT = 3
TILE = 16
SUBLANES = 8
VMEM_BYTES = 65000 * 1024

spectral_scale = 8.5
beta_coef = 0.6
chem_level = 1.0
coupling = 1.0
density_floor = 0.05

MESH = pl.DeviceIdType.MESH


def quotient(value, by):
    return lax.div(value, jnp.int32(by))


def modulo(value, by):
    return lax.rem(value, jnp.int32(by))


def round_up(value, step):
    return -(-value // step) * step


def plan(n_cuts, n_slab, cap, flat):
    groups = 2 if cap % 2 == 0 and n_slab % 2 == 0 else 1
    pieces = n_slab // groups
    total = flat // (NX * PACK)
    core = total // pieces
    halo = -(-DEGREE // PACK)
    width = min(round_up(core + halo, TILE), total)
    windows = (total - width) // SUBLANES + 1
    for piece in range(pieces):
        low, high = max(piece * core - halo, 0), min((piece + 1) * core + halo, total)
        start = SUBLANES * min(low // SUBLANES, windows - 1)
        assert start <= low and high <= start + width
    return groups, pieces, core, width, windows


def for_planes(count, body):
    chunk = 4 if count % 4 == 0 else 1
    if count == chunk:
        for z in range(chunk):
            body(z)
        return

    def some(i, carry):
        for z in range(chunk):
            body(i * chunk + z)
        return carry

    lax.fori_loop(0, count // chunk, some, 0)


def to_rows(flat_rows):
    p0, p1, p2 = flat_rows
    lane = lax.broadcasted_iota(jnp.int32, p0.shape, 1)
    r0, r1 = pltpu.roll(p0, 32, 1), pltpu.roll(p1, 32, 1)
    s1, s2 = pltpu.roll(p1, 64, 1), pltpu.roll(p2, 64, 1)
    rows = [
        p0,
        jnp.where(lane < 32, r0, r1),
        jnp.where(lane < 64, s1, s2),
        pltpu.roll(p2, 96, 1),
    ]
    return [jnp.where(lane < NX, row, 0.0) for row in rows]


def kernel(
    dims,
    counts_in,
    slot_slice_in,
    occupation_in,
    coef_in,
    table_in,
    index_in,
    mean_in,
    pairing_in,
    vectors,
    out,
    counts,
    slot_slice,
    occupation,
    coef,
    table,
    index_here,
    mean_here,
    pairing_here,
    local_rows,
    fields,
    got_q,
    got_f,
    wide,
    q_rows,
    ab,
    even,
    odd,
    dens,
    sibling,
    parts,
    landed,
    load_sem,
    q_send,
    q_recv,
    f_send,
    f_recv,
    s_send,
    s_recv,
    p_send,
    p_recv,
):
    n_cuts, nz, groups, pieces, core, width, windows, per_group, share_rows = dims
    cut, slab = lax.axis_index("cuts"), lax.axis_index("slab")
    near = n_cuts // pieces
    turn = max(near // 2, 1)
    home = quotient(cut, near)
    cap = per_group * groups
    kept = nz // groups
    halo = -(-DEGREE // PACK)

    def piece_of(s):
        return modulo(quotient(s, groups) + quotient(cut, turn), pieces)

    def window_of(p):
        low = jnp.maximum(p * core - halo, 0)
        return jnp.minimum(quotient(low, SUBLANES), windows - 1)

    piece, group = piece_of(slab), modulo(slab, groups)
    keeps_own = (home == piece).astype(jnp.int32)

    others = [modulo(slab + o, nz) for o in range(1, nz)]
    barrier = pltpu.get_barrier_semaphore()
    for to in others:
        pl.semaphore_signal(barrier, inc=1, device_id=(cut, to), device_id_type=MESH)

    loads = [
        pltpu.make_async_copy(src, dst, load_sem.at[i])
        for i, (src, dst) in enumerate(
            [
                (index_in, index_here),
                (table_in, table),
                (mean_in, mean_here),
                (pairing_in, pairing_here),
                (counts_in, counts),
                (slot_slice_in, slot_slice),
                (occupation_in, occupation),
                (coef_in, coef),
            ]
        )
    ]
    for load in loads[:4]:
        load.start()

    def source_slab(c):
        return modulo(home + pieces * n_cuts - quotient(c, turn), pieces) * groups + group

    for o in range(n_cuts):
        c = modulo(cut + o, n_cuts)
        s = source_slab(c)

        def greet(c=c, s=s):
            pl.semaphore_signal(barrier, inc=1, device_id=(c, s), device_id_type=MESH)

        if o:
            greet()
        else:
            pl.when(s != slab)(greet)

    for load in loads[:4]:
        load.wait()
    hits = index_here[...]
    trap = jnp.zeros(hits.shape, jnp.float32)
    for level in range(table.shape[0]):
        trap = jnp.where(hits == level, table[level], trap)
    fields[0] = (2.0 / spectral_scale) * (3.0 + (trap + mean_here[...]))
    fields[1] = (2.0 / spectral_scale) * pairing_here[...]

    pl.semaphore_wait(barrier, nz - 1 + near * kept - keeps_own)

    mate = slab + 1 - 2 * group

    def passed_on(src):
        return pltpu.make_async_remote_copy(
            src_ref=got_f.at[src],
            dst_ref=got_f.at[src],
            send_sem=f_send.at[nz + src],
            recv_sem=f_recv.at[src],
            device_id=(cut, mate),
            device_id_type=MESH,
        )

    def field_copy(to):
        start = pl.multiple_of(window_of(piece_of(to)) * (SUBLANES * FLAT), SUBLANES)
        return pltpu.make_async_remote_copy(
            src_ref=fields.at[:, pl.ds(start, width * FLAT)],
            dst_ref=got_f.at[slab],
            send_sem=f_send.at[to],
            recv_sem=f_recv.at[slab],
            device_id=(cut, to),
            device_id_type=MESH,
        )

    def vector_copy(to, slot):
        start = window_of(piece_of(to)) * (SUBLANES * FLAT)
        return pltpu.make_async_remote_copy(
            src_ref=vectors.at[modulo(to, groups) * per_group + slot, pl.ds(start, width * FLAT)],
            dst_ref=got_q.at[slot, slab],
            send_sem=q_send.at[slot, to],
            recv_sem=q_recv.at[slot, slab],
            device_id=(cut, to),
            device_id_type=MESH,
        )

    window = window_of(piece)
    alike = [modulo(slab + o, nz) for o in range(groups, nz, groups)]
    direct = alike + ([mate] if groups > 1 else [])
    for to in direct:
        field_copy(to).start()
    for to in others:
        vector_copy(to, 0).start()
    own_start = pl.multiple_of(window * (SUBLANES * FLAT), SUBLANES)
    own_f = pltpu.make_async_copy(
        fields.at[:, pl.ds(own_start, width * FLAT)], got_f.at[slab], f_recv.at[slab]
    )
    own_f.start()

    def own_q(slot):
        return pltpu.make_async_copy(
            vectors.at[group * per_group + slot, pl.ds(own_start, width * FLAT)],
            got_q.at[slot, slab],
            q_recv.at[slot, slab],
        )

    own_q(0).start()
    for slot in range(1, per_group):
        for to in others:
            vector_copy(to, slot).start()
        own_q(slot).start()
    for load in loads[4:]:
        load.start()

    lane = lax.broadcasted_iota(jnp.int32, (width, LANES), 1)
    line = lax.broadcasted_iota(jnp.int32, (width, LANES), 0)
    not_first, not_last = line > 0, line < width - 1
    hop = jnp.where(lane < NX, -1.0 / spectral_scale, 0.0).astype(jnp.float32)

    blank = jnp.zeros((2, PACK, width, LANES), jnp.float32)
    for buffer in (even, odd):
        buffer[:, 0] = blank
        buffer[:, nz + 1] = blank
    dens[...] = jnp.zeros(dens.shape, jnp.float32)

    def wait_fields(src):
        pltpu.make_async_remote_copy(
            src_ref=fields.at[:, pl.ds(own_start, width * FLAT)],
            dst_ref=got_f.at[src],
            send_sem=f_send.at[src],
            recv_sem=f_recv.at[src],
            device_id=(cut, src),
            device_id_type=MESH,
        ).wait_recv()

    for src in alike:
        wait_fields(src)
        if groups > 1:
            passed_on(src).start()
    own_f.wait()
    if groups > 1:
        wait_fields(mate)
        for src in alike:
            wait_fields(src + 1 - 2 * group)

    for load in loads[4:]:
        load.wait()

    def unpack_fields(z):
        for which in range(2):
            rows = to_rows(
                [got_f[z, which, pl.ds(j, width, stride=FLAT)] for j in range(FLAT)]
            )
            for i in range(PACK):
                ab[which, z, i] = rows[i]

    for_planes(nz, unpack_fields)

    def beside(ref, part, z):
        rows = [ref[part, z + 1, i] for i in range(PACK)]
        above = jnp.where(not_first, pltpu.roll(rows[-1], 1, 0), 0.0)
        below = jnp.where(not_last, pltpu.roll(rows[0], width - 1, 0), 0.0)
        padded = [above] + rows + [below]
        sums = []
        for i in range(PACK):
            around = pltpu.roll(rows[i], 1, 1) + pltpu.roll(rows[i], LANES - 1, 1)
            around = around + (padded[i] + padded[i + 2])
            if not (isinstance(z, int) and z == 0):
                around = around + ref[part, z, i]
            if not (isinstance(z, int) and z == nz - 1):
                around = around + ref[part, z + 2, i]
            sums.append(hop * around)
        return rows, sums

    def twice_operator(ref, z):
        u, near_u = beside(ref, 0, z)
        v, near_v = beside(ref, 1, z)
        results = []
        for i in range(PACK):
            a, b = ab[0, z, i], ab[1, z, i]
            results.append((a * u[i] + b * v[i] + near_u[i], b * u[i] - a * v[i] - near_v[i]))
        return results

    def clenshaw(now, then, scale, first=False):
        def plane(z):
            for i, pair in enumerate(twice_operator(now, z)):
                for part in range(2):
                    value = scale * q_rows[part, z, i] + pair[part]
                    if not first:
                        value = value - then[part, z + 1, i]
                    then[part, z + 1, i] = value

        for_planes(nz, plane)

    def sibling_copy(k):
        return pltpu.make_async_remote_copy(
            src_ref=dens.at[groups * k + 1 - group],
            dst_ref=sibling.at[k],
            send_sem=s_send.at[k],
            recv_sem=s_recv.at[k],
            device_id=(cut, mate),
            device_id_type=MESH,
        )

    def one_slot(slot, carry):
        own_q(slot).wait()
        for src in others:
            pltpu.make_async_remote_copy(
                src_ref=vectors.at[slot, pl.ds(own_start, width * FLAT)],
                dst_ref=got_q.at[slot, src],
                send_sem=q_send.at[slot, src],
                recv_sem=q_recv.at[slot, src],
                device_id=(cut, src),
                device_id_type=MESH,
            ).wait_recv()
        index = group * per_group + slot
        number = cut * cap + index
        level = slot_slice[number]
        weight = jnp.where(index < counts[cut], occupation[number], 0.0)
        last = coef[level, DEGREE]

        def unpack(z):
            for r in range(width * FLAT):
                wide[z, pl.ds(2 * r, 2)] = got_q[slot, z, r].astype(jnp.float32)
            for part in range(2):
                flat = [
                    wide[z, pl.ds(2 * j + part, width, stride=2 * FLAT)] for j in range(FLAT)
                ]
                rows = to_rows(flat)
                for i in range(PACK):
                    q_rows[part, z, i] = rows[i]
                    even[part, z + 1, i] = last * rows[i]

        for_planes(nz, unpack)
        clenshaw(even, odd, coef[level, DEGREE - 1], first=True)

        def two_steps(k, inner):
            order = DEGREE - 2 - 2 * k
            clenshaw(odd, even, coef[level, order])
            clenshaw(even, odd, coef[level, order - 1])
            return inner

        lax.fori_loop(0, (DEGREE - 2) // 2, two_steps, 0)
        base = coef[level, 0]

        def finish(z):
            for i, pair in enumerate(twice_operator(odd, z)):
                f = [
                    base * q_rows[part, z, i] + 0.5 * pair[part] - even[part, z + 1, i]
                    for part in range(2)
                ]
                heavy = weight * f[1]
                dens[z, 0, i] += heavy * f[1]
                dens[z, 1, i] += heavy * f[0]

        if groups == 1:
            for_planes(nz, finish)
            return carry
        for k in range(kept):
            finish(groups * k + 1 - group)
            pl.when(slot == per_group - 1)(sibling_copy(k).start)
        for k in range(kept):
            finish(groups * k + group)
        return carry

    lax.fori_loop(0, per_group, one_slot, 0)

    inside = piece * core - window * SUBLANES
    def part_copy(c, k):
        return pltpu.make_async_remote_copy(
            src_ref=parts.at[c, k],
            dst_ref=landed.at[cut],
            send_sem=p_send.at[c, k],
            recv_sem=p_recv.at[cut],
            device_id=(piece * near + c, groups * k + group),
            device_id_type=MESH,
        )

    def elsewhere(c, k):
        return jnp.logical_or(piece * near + c != cut, groups * k + group != slab)

    def pack(c, k):
        z = groups * k + group
        if share_rows % PACK == 0:
            step = share_rows // PACK
            spans = [(i, i, c * step, step) for i in range(PACK)]
        else:
            rows = [(r, c * share_rows + r) for r in range(share_rows)]
            spans = [(r, y % PACK, y // PACK, 1) for r, y in rows]
        for which in range(2):
            for r, i, g, n in spans:
                value = dens[z, which, i, pl.ds(inside + g, n)]
                if groups > 1:
                    value = value + sibling[k, which, i, pl.ds(inside + g, n)]
                if n == 1:
                    parts[c, k, pl.ds(which * share_rows + r, 1)] = value
                else:
                    parts[c, k, pl.ds(which * share_rows + r, n, stride=PACK)] = value

    for k in range(kept):
        if groups > 1:
            sibling_copy(k).wait_recv()
        for c in range(near):
            pack(c, k)
        for c in range(near):
            pl.when(elsewhere(c, k))(part_copy(c, k).start)

    @pl.when(home == piece)
    def _():
        landed[cut] = parts[modulo(cut, near), quotient(slab, groups)]

    for part, here in enumerate((mean_here, pairing_here)):
        count = here.shape[0] // FLAT
        rows = to_rows([here[pl.ds(j, count, stride=FLAT)] for j in range(FLAT)])
        for i in range(PACK):
            local_rows[part, i] = rows[i]
        for r in range(share_rows):
            y = cut * share_rows + r
            out[part, pl.ds(2 * share_rows + r, 1)] = local_rows[
                part, modulo(y, PACK), pl.ds(quotient(y, PACK), 1)
            ]

    for to in direct:
        field_copy(to).wait_send()
    if groups > 1:
        for src in alike:
            passed_on(src).wait_send()
    for to in others:
        for slot in range(per_group):
            vector_copy(to, slot).wait_send()
    for o in range(n_cuts):
        c = modulo(cut + o, n_cuts)

        def arrive(c=c):
            pltpu.make_async_remote_copy(
                src_ref=parts.at[0, 0],
                dst_ref=landed.at[c],
                send_sem=p_send.at[0, 0],
                recv_sem=p_recv.at[c],
                device_id=(c, source_slab(c)),
                device_id_type=MESH,
            ).wait_recv()

        if o:
            arrive()
        else:
            pl.when(source_slab(c) != slab)(arrive)
    half = n_cuts // 2
    for i, some in enumerate((range(half), range(half, n_cuts))):
        total = jnp.zeros(landed.shape[1:], jnp.float32)
        for source in some:
            total = total + landed[source]
        out[i, pl.ds(0, 2 * share_rows)] = total[: 2 * share_rows]

    for k in range(kept):
        if groups > 1:
            sibling_copy(k).wait_send()
        for c in range(near):
            pl.when(elsewhere(c, k))(part_copy(c, k).wait_send)


def body(
    quasi, counts, slot_slice, occupation, filter_coef, trap_index, trap_table, mean_field, pairing
):
    n_cuts, nz = lax.axis_size("cuts"), lax.axis_size("slab")
    cap, flat = quasi.shape[1], quasi.shape[3]
    share = flat // n_cuts
    share_rows = share // NX
    groups, pieces, core, width, windows = plan(n_cuts, nz, cap, flat)
    per_group = cap // groups
    vectors = quasi.reshape(2, cap, flat // LANES, LANES).transpose(1, 2, 0, 3)

    rows = round_up(2 * share_rows, SUBLANES)
    near = n_cuts // pieces
    kept = nz // groups
    dims = (n_cuts, nz, groups, pieces, core, width, windows, per_group, share_rows)
    f32, i32 = jnp.float32, jnp.int32
    tall = (flat // LANES, LANES)
    slots = slot_slice.shape[0]
    sums = pl.pallas_call(
        functools.partial(kernel, dims),
        out_shape=pltpu.VMEM((2, 3 * share_rows, LANES), f32),
        in_specs=[pl.BlockSpec(memory_space=pltpu.HBM)] * 8
        + [pl.BlockSpec(memory_space=pl.ANY)],
        out_specs=pl.BlockSpec(memory_space=pltpu.VMEM),
        scratch_shapes=[
            pltpu.SMEM((n_cuts,), i32),
            pltpu.SMEM((slots,), i32),
            pltpu.SMEM((slots,), f32),
            pltpu.SMEM(filter_coef.shape, f32),
            pltpu.SMEM(trap_table.shape, f32),
            pltpu.VMEM(tall, i32),
            pltpu.VMEM(tall, f32),
            pltpu.VMEM(tall, f32),
            pltpu.VMEM((2, PACK, flat // (NX * PACK), LANES), f32),
            pltpu.VMEM((2, *tall), f32),
            pltpu.VMEM((per_group, nz, FLAT * width, 2, LANES), jnp.bfloat16),
            pltpu.VMEM((nz, 2, FLAT * width, LANES), f32),
            pltpu.VMEM((nz, 2 * FLAT * width, LANES), f32),
            pltpu.VMEM((2, nz, PACK, width, LANES), f32),
            pltpu.VMEM((2, nz, PACK, width, LANES), f32),
            pltpu.VMEM((2, nz + 2, PACK, width, LANES), f32),
            pltpu.VMEM((2, nz + 2, PACK, width, LANES), f32),
            pltpu.VMEM((nz, 2, PACK, width, LANES), f32),
            pltpu.VMEM((kept, 2, PACK, width, LANES), f32),
            pltpu.VMEM((near, kept, rows, LANES), f32),
            pltpu.VMEM((n_cuts, rows, LANES), f32),
            pltpu.SemaphoreType.DMA((8,)),
            pltpu.SemaphoreType.DMA((per_group, nz)),
            pltpu.SemaphoreType.DMA((per_group, nz)),
            pltpu.SemaphoreType.DMA((2 * nz,)),
            pltpu.SemaphoreType.DMA((nz,)),
            pltpu.SemaphoreType.DMA((kept,)),
            pltpu.SemaphoreType.DMA((kept,)),
            pltpu.SemaphoreType.DMA((near, kept)),
            pltpu.SemaphoreType.DMA((n_cuts,)),
        ],
        compiler_params=pltpu.CompilerParams(
            collective_id=0, has_side_effects=True, vmem_limit_bytes=VMEM_BYTES
        ),
    )(
        counts,
        slot_slice,
        occupation,
        filter_coef,
        trap_table,
        trap_index.reshape(tall),
        mean_field.reshape(tall),
        pairing.reshape(tall),
        vectors,
    )

    halves = sums[:, :, :NX].reshape(6, share)
    normal_density = halves[0:1] + halves[3:4]
    anomalous_density = halves[1:2] + halves[4:5]
    mean_local, pairing_local = halves[2:3], halves[5:6]
    cube_root = jnp.cbrt(normal_density + density_floor)
    new_mean_field = 0.5 * mean_local + 0.5 * (beta_coef * cube_root * cube_root - chem_level)
    new_pairing = 0.5 * pairing_local - coupling * anomalous_density
    return (normal_density, anomalous_density, new_mean_field, new_pairing)


def solution(mesh):
    return jax.shard_map(
        body,
        mesh=mesh,
        in_specs=(
            P(None, "cuts", "slab", None),
            P(),
            P(),
            P(),
            P(),
            P("slab", None),
            P(),
            P("slab", None),
            P("slab", None),
        ),
        out_specs=(P("slab", "cuts"), P("slab", "cuts"), P("slab", "cuts"), P("slab", "cuts")),
        check_vma=False,
    )
```
